32 devices in a mesh: dp: 8 (over y, x, core), tensor: 4 (over z).
Axes of the slice: x: 2, y: 2, z: 4, core: 2. Of those that a mesh axis runs over, the one named last changes fastest.
Arguments:
- tokens: bfloat16 [2048, 8, 1024], P('tensor', 'dp'), may hold values from -6 to 6
- qkv_weight: bfloat16 [1024, 3, 1024], P(None, None, 'tensor'), may hold values from -0.1875 to 0.1875
- output_projection_weight: bfloat16 [1024, 1024], P('tensor'), may hold values from -4 to 4
- gate_up_weight: bfloat16 [1024, 2, 4096], P(None, None, 'tensor'), may hold values from -0.1875 to 0.1875
- down_projection_weight: bfloat16 [4096, 1024], P('tensor'), may hold values from -0.09375 to 0.09375
- attention_gain: float32 [1024], replicated, may hold values from 0.1 to 1.9
- feedforward_gain: float32 [1024], replicated, may hold values from 0.1 to 1.9
- window_lengths: int32 [8], P('dp'), may hold values from 512 to 2048, as said below
- key_mask: int32 [2048, 8], P(None, 'dp'), may hold values from 0 to 1, as said below
- cotangent: bfloat16 [2048, 8, 1024], P('tensor', 'dp'), may hold values from -12 to 12
Outputs:
- output: bfloat16 [2048, 8, 1024], P('tensor', 'dp')
- tokens_grad: bfloat16 [2048, 8, 1024], P('tensor', 'dp')
- qkv_grad: float32 [1024, 3, 1024], P(None, None, 'tensor')
- out_grad: float32 [1024, 1024], P('tensor')
- gate_up_grad: float32 [1024, 2, 4096], P(None, None, 'tensor')
- down_projection_gradient: float32 [4096, 1024], P('tensor')
- attention_gain_grad: float32 [1024], replicated
- feedforward_gain_grad: float32 [1024], replicated
The draws below stay inside these ranges and needn't reach their ends.
Inputs may be any that keep to these rules, and one draw needn't show every extreme that they name: `window_lengths`: among the 1 windows of each index of dp, one drawn from the seed has length 2048. `key_mask`: slot 0 of every window is 1.
All inputs are finite; a program needn't handle non-finite values.
Results may differ from the reference program's by a relative error of at most 0.02.
Values may be sent and summed in bfloat16 or wider, within the bound.
No kernel may reach another device: no remote copies, remote signals or barrier semaphores. Data moves between devices by JAX's collectives and lax.ppermute only.
A program may use at most 384 MiB of HBM per device.

```python
import jax
import jax.numpy as jnp
from jax import lax

D = 1024
HEADS = 16
HEAD_DIM = 64
FF = 4096
LEN = 2048
SEQ_DP = 1
SEQS = 8


def draw_window_lengths(key, part):
    key = jax.random.fold_in(key, 5)
    first_key, second_key = jax.random.split(key)
    drawn_lengths = jax.random.randint(first_key, (SEQS,), LEN // 4, LEN + 1)
    groups = SEQS // SEQ_DP
    chosen = jax.random.randint(second_key, (groups,), 0, SEQ_DP)
    slot_index = jnp.arange(SEQS, dtype=jnp.int32) % SEQ_DP
    longest = slot_index == jnp.repeat(chosen, SEQ_DP)
    return jnp.where(longest, LEN, drawn_lengths).astype(jnp.int32)


def draw_key_mask(key, part):
    key = jax.random.fold_in(key, 7)
    levels = jax.random.randint(key, (LEN, SEQS), 0, 8)
    first_row = (jnp.arange(LEN, dtype=jnp.int32) == 0)[:, None]
    return jnp.where(first_row | (levels != 0), 1, 0).astype(jnp.int32)


def draw_cotangent(key, part):
    key = jax.random.fold_in(key, 11)
    base_key = jax.random.fold_in(key, 0)
    seq_ramp = 3.0 ** (jnp.arange(SEQS, dtype=jnp.float32) / max(SEQS - 1, 1))
    noise_field = jax.random.normal(base_key, (LEN, SEQS, D), dtype=jnp.float32)
    return (jnp.clip(noise_field, -4.0, 4.0) * seq_ramp[None, :, None]).astype(jnp.bfloat16)


def block_levels(own_key, shape, cuts, low, top_value):
    level = 1.0
    for axis_at, blocks in cuts:
        draws = jax.random.uniform(jax.random.fold_in(jax.random.fold_in(own_key, 6), axis_at), (blocks,), jnp.float32, low / len(cuts), top_value / len(cuts))
        level = level * jnp.repeat(jnp.exp(draws), shape[axis_at] // blocks).reshape((-1,) + (1,) * (len(shape) - 1 - axis_at))
    return level


def noise(own_key, extent, spread, most, cuts=(), held_as=jnp.bfloat16):
    values = jax.random.normal(own_key, extent, jnp.float32) * spread
    if len(cuts) > 0:
        values = block_levels(own_key, extent, cuts, -0.22, 0.18) * values
    return jnp.clip(values, min=-most, max=most).astype(held_as)


def setup_inputs(seed: int = 0) -> dict:
    splits = jax.random.split(jax.random.key(seed), 11)
    tokens = noise(splits[0], (LEN, SEQS, D), 1.0, 6.0, ((0, 4), (1, 8)))
    qkv_weight = noise(splits[1], (D, 3, D), D ** -0.5, 0.1875, ((2, 4),))
    output_projection_weight = noise(splits[2], (D, D), (max(1, 4 * D // LEN)) ** -0.5, 4.0, ((0, 4),))
    gate_up_weight = noise(splits[3], (D, 2, FF), D ** -0.5, 0.1875, ((2, 4),))
    down_projection_weight = noise(splits[4], (FF, D), FF ** -0.5, 0.09375, ((0, 4),))
    attention_gain = jnp.clip(1.0 + 0.18 * jax.random.normal(splits[5], (D,), jnp.float32), 0.1, 1.9)
    feedforward_gain = jnp.clip(1.0 + 0.18 * jax.random.normal(splits[6], (D,), jnp.float32), 0.1, 1.9)
    window_lengths = draw_window_lengths(jax.random.fold_in(splits[10], 71), 0)
    key_mask = draw_key_mask(jax.random.fold_in(splits[10], 71), 0)
    cotangent = draw_cotangent(jax.random.fold_in(splits[10], 71), 0)
    return dict(tokens=tokens, qkv_weight=qkv_weight, output_projection_weight=output_projection_weight, gate_up_weight=gate_up_weight, down_projection_weight=down_projection_weight, attention_gain=attention_gain, feedforward_gain=feedforward_gain, window_lengths=window_lengths, key_mask=key_mask, cotangent=cotangent)


EPSILON = 1e-05
MASKED = -1000000000.0
ROPE_BASE = 10000.0
HIGHEST = lax.Precision.HIGHEST

@jax.custom_vjp
def low(v):
    return lax.optimization_barrier(v.astype(jnp.bfloat16)).astype(jnp.float32)

@jax.custom_vjp
def low_back(v):
    return v

def low_keep(v):
    return (low(v), None)

def low_pass(kept, grad):
    return (grad,)

def back_keep(v):
    return (v, None)

def back_low(kept, grad):
    return (low(grad),)
low.defvjp(low_keep, low_pass)
low_back.defvjp(back_keep, back_low)

def layer_norm(rows, gains):
    average = lax.optimization_barrier(jnp.mean(rows, axis=-1, keepdims=True))
    centered = rows - average
    variance = lax.optimization_barrier(jnp.mean(centered * centered, axis=-1, keepdims=True))
    return centered * lax.rsqrt(variance + EPSILON) * gains

def rope_tables():
    midpoint = HEAD_DIM // 2
    frequencies = ROPE_BASE ** (-(jnp.arange(midpoint, dtype=jnp.float32) * 2.0 / HEAD_DIM))
    angles = jnp.arange(LEN, dtype=jnp.float32)[:, None] * frequencies[None, :]
    angles = jnp.concatenate([angles, angles], axis=1)
    return (jnp.cos(angles), jnp.sin(angles))

def rotate_half(values):
    midpoint = values.shape[-1] // 2
    return jnp.concatenate([-values[..., midpoint:], values[..., :midpoint]], axis=-1)

def turn(values, cosines, sines):
    return values * cosines[:, None, :] + rotate_half(values) * sines[:, None, :]

def head_attention(item, valid):
    query_rows, key_rows, value_rows = item
    scores = low_back(jnp.dot(query_rows, key_rows.T, precision=HIGHEST) * HEAD_DIM ** (-0.5))
    scores = jnp.where(valid[None, :], scores, MASKED)
    row_max = lax.optimization_barrier(jnp.max(scores, axis=1, keepdims=True))
    exp_rows = jnp.exp(scores - row_max)
    prob_rows = exp_rows / lax.optimization_barrier(jnp.sum(exp_rows, axis=1, keepdims=True))
    return jnp.dot(low(prob_rows), value_rows, precision=HIGHEST)

def layer_window(item, qkv_weight, output_projection_weight, gate_up_weight, down_projection_weight, attention_gain, feedforward_gain):
    window, valid = item
    cosines, sines = rope_tables()
    normed_attn = low(layer_norm(window, attention_gain))
    projected = low_back(jnp.einsum('ld,dcf->lcf', normed_attn, qkv_weight, precision=HIGHEST))
    head_shape = (LEN, HEADS, HEAD_DIM)
    queries = low(turn(projected[:, 0].reshape(head_shape), cosines, sines))
    keys_all = low(turn(projected[:, 1].reshape(head_shape), cosines, sines))
    values_all = low(projected[:, 2].reshape(head_shape))

    def one_head(head_item):
        return head_attention(head_item, valid)
    per_head = lax.map(jax.checkpoint(one_head), (queries.transpose(1, 0, 2), keys_all.transpose(1, 0, 2), values_all.transpose(1, 0, 2)))
    heads_out = low(low_back(per_head)).transpose(1, 0, 2).reshape(LEN, D)
    attn_branch = low_back(jnp.dot(heads_out, output_projection_weight, precision=HIGHEST))
    middle = window + attn_branch
    normed_ffn = low(layer_norm(middle, feedforward_gain))
    gate_up = low_back(jnp.einsum('ld,dcf->lcf', normed_ffn, gate_up_weight, precision=HIGHEST))
    gate_part = gate_up[:, 0]
    hidden_state = low(gate_part * jax.nn.sigmoid(gate_part) * gate_up[:, 1])
    ffn_branch = low_back(jnp.dot(hidden_state, down_projection_weight, precision=HIGHEST))
    return middle + ffn_branch

def reference(tokens, qkv_weight, output_projection_weight, gate_up_weight, down_projection_weight, attention_gain, feedforward_gain, window_lengths, key_mask, cotangent):
    positions = jnp.arange(LEN, dtype=jnp.int32)
    valid = (positions[:, None] < window_lengths[None, :]) & (key_mask == 1)

    def forward(tokens_f, qkv_f, out_f, gate_up_f, down_f, attention_f, feedforward_f):

        def one_window(item):
            return layer_window(item, qkv_f, out_f, gate_up_f, down_f, attention_f, feedforward_f)
        result = lax.map(jax.checkpoint(one_window), (jnp.moveaxis(tokens_f, 1, 0), jnp.moveaxis(valid, 1, 0)))
        return jnp.moveaxis(result, 0, 1)
    output, pullback = jax.vjp(forward, tokens.astype(jnp.float32), qkv_weight.astype(jnp.float32), output_projection_weight.astype(jnp.float32), gate_up_weight.astype(jnp.float32), down_projection_weight.astype(jnp.float32), attention_gain.astype(jnp.float32), feedforward_gain.astype(jnp.float32))
    grads = pullback(cotangent.astype(jnp.float32))
    return (output.astype(jnp.bfloat16), grads[0].astype(jnp.bfloat16), grads[1], grads[2], grads[3], grads[4], grads[5], grads[6])
```

```python
import functools
import math

import jax
import jax.numpy as jnp
from jax import lax
from jax.experimental import pallas as pl
from jax.experimental.pallas import tpu as pltpu
from jax.sharding import PartitionSpec as P

HEAD_DIM = 64
EPSILON = 1e-05
MASKED = -1000000000.0
ROPE_BASE = 10000.0
LOG2E = math.log2(math.e)
SCALE = HEAD_DIM ** (-0.5)
BF16 = jnp.bfloat16
F32 = jnp.float32
MIB = 1 << 20


def dot(a, b, ca, cb):
    return lax.dot_general(a, b, (((ca,), (cb,)), ((), ())), preferred_element_type=F32)


def call(body, name, out, vmem=56, flops=0, moved=0, **kw):
    return pl.pallas_call(
        body,
        out_shape=out,
        name=name,
        compiler_params=pltpu.CompilerParams(vmem_limit_bytes=vmem * MIB),
        cost_estimate=pl.CostEstimate(flops=flops, bytes_accessed=moved, transcendentals=0),
        **kw,
    )


def shape(s, d):
    return jax.ShapeDtypeStruct(s, d)


def norm_rows(x, gain):
    centered = x - jnp.mean(x, axis=-1, keepdims=True)
    inverse = lax.rsqrt(jnp.mean(centered * centered, axis=-1, keepdims=True) + EPSILON)
    scaled = centered * inverse
    return scaled * gain, scaled, inverse


def norm_kernel(x_ref, g_ref, o_ref):
    o_ref[...] = norm_rows(x_ref[...].astype(F32), g_ref[...])[0].astype(BF16)


def norm_call(x, gain):
    n, d = x.shape
    b = min(128, n)
    return call(
        norm_kernel,
        "norm_tokens",
        shape((n, d), BF16),
        grid=(n // b,),
        in_specs=[pl.BlockSpec((b, d), lambda i: (i, 0)), pl.BlockSpec((1, d), lambda i: (0, 0))],
        out_specs=pl.BlockSpec((b, d), lambda i: (i, 0)),
        flops=12 * n * d,
        moved=4 * n * d,
    )(x, gain)


def middle_kernel(x_ref, g_ref, *refs):
    parts, (m_ref, o_ref) = refs[:-2], refs[-2:]
    m = x_ref[...].astype(F32)
    for p in parts:
        m = m + p[...].astype(F32)
    m_ref[...] = m
    o_ref[...] = norm_rows(m, g_ref[...])[0].astype(BF16)


def middle_call(x, gain, parts):
    n, d = x.shape
    b = min(128, n)
    row = pl.BlockSpec((b, d), lambda i: (i, 0))
    return call(
        middle_kernel,
        "middle_norm",
        (shape((n, d), F32), shape((n, d), BF16)),
        grid=(n // b,),
        in_specs=[row, pl.BlockSpec((1, d), lambda i: (0, 0))] + [row] * len(parts),
        out_specs=(row, row),
        flops=12 * n * d,
        moved=10 * n * d,
    )(x, gain, *parts)


def back_kernel(n_parts, keep, base_ref, x_ref, g_ref, *refs):
    parts, outs = refs[:n_parts], refs[n_parts:]
    e = parts[0][...].astype(F32)
    for p in parts[1:]:
        e = e + p[...].astype(F32)
    gain = g_ref[...]
    _, scaled, inverse = norm_rows(x_ref[...].astype(F32), gain)
    through = e * gain
    first = jnp.mean(through, axis=-1, keepdims=True)
    second = jnp.mean(through * scaled, axis=-1, keepdims=True)
    total = base_ref[...].astype(F32) + inverse * (through - first - scaled * second)
    if keep:
        outs[0][...] = total
    outs[-2][...] = total.astype(BF16)

    @pl.when(pl.program_id(0) == 0)
    def _():
        outs[-1][...] = jnp.zeros_like(outs[-1])

    outs[-1][...] += jnp.sum(e * scaled, axis=0, keepdims=True)


def back_call(name, base, x, gain, parts, keep):
    n, d = x.shape
    b = min(128, n)
    row = pl.BlockSpec((b, d), lambda i: (i, 0))
    one = pl.BlockSpec((1, d), lambda i: (0, 0))
    out = [shape((n, d), F32)] * keep + [shape((n, d), BF16), shape((1, d), F32)]
    return call(
        functools.partial(back_kernel, len(parts), keep),
        name,
        tuple(out),
        grid=(n // b,),
        in_specs=[row, row, one] + [row] * len(parts),
        out_specs=tuple([row] * (keep + 1) + [one]),
        flops=25 * n * d,
        moved=12 * n * d,
    )(base, x, gain, *parts)


def output_kernel(m_ref, *refs):
    total = m_ref[...]
    for p in refs[:-1]:
        total = total + p[...].astype(F32)
    refs[-1][...] = total.astype(BF16)


def output_call(m, parts):
    n, d = m.shape
    b = min(256, n)
    row = pl.BlockSpec((b, d), lambda i: (i, 0))
    return call(
        output_kernel,
        "output_sum",
        shape((n, d), BF16),
        grid=(n // b,),
        in_specs=[row] * (1 + len(parts)),
        out_specs=row,
        flops=4 * n * d,
        moved=10 * n * d,
    )(m, *parts)


def turn(u, cos, sin):
    half = HEAD_DIM // 2
    first, second = u[:half], u[half:]
    return jnp.concatenate([first * cos - second * sin, second * cos + first * sin], axis=0)


def turn_back(u, cos, sin):
    half = HEAD_DIM // 2
    first, second = u[:half], u[half:]
    return jnp.concatenate([first * cos + second * sin, second * cos - first * sin], axis=0)


def qkv_kernel(n_parts, c_ref, s_ref, w_ref, *refs):
    parts, (q_ref, k_ref, v_ref) = refs[:n_parts], refs[n_parts:]
    n = parts[0].shape[0]
    for i, p in enumerate(parts):
        cols = slice(i * n, (i + 1) * n)
        cos, sin = c_ref[:, cols], s_ref[:, cols]
        for which, out in enumerate((q_ref, k_ref, v_ref)):
            u = dot(w_ref[which], p[...], 0, 1)
            for h in range(u.shape[0] // HEAD_DIM):
                rows = slice(h * HEAD_DIM, (h + 1) * HEAD_DIM)
                head = u[rows]
                if which < 2:
                    head = turn(head, cos, sin)
                out[rows, cols] = head.astype(BF16)


def qkv_call(parts, w, cos, sin):
    n, d = parts[0].shape
    f = w.shape[2]
    total = n * len(parts)
    return call(
        functools.partial(qkv_kernel, len(parts)),
        "project_heads",
        (shape((f, total), BF16),) * 3,
        flops=6 * f * d * total,
        moved=2 * (total * d + 3 * d * f + 3 * f * total),
    )(cos, sin, w, *parts)


def split(x, n):
    out = []
    for _ in range(n):
        h = x.astype(BF16)
        out.append(h)
        x = x - h.astype(F32)
    return out


def attend_kernel(q_ref, k_ref, v_ref, b_ref, o_ref, l_ref, ka, va, *, sub):
    S = k_ref.shape[1]
    bq = q_ref.shape[1]

    @pl.when(pl.program_id(1) == 0)
    def _():
        k = k_ref[...]
        ka[...] = jnp.concatenate([k, k, b_ref[...]], axis=0).T
        va[0:HEAD_DIM] = v_ref[...]
        va[HEAD_DIM:] = jnp.ones((16, S), BF16)

    high, low = split(q_ref[...].astype(F32) * (SCALE * LOG2E), 2)
    row = lax.broadcasted_iota(jnp.int32, (16, bq), 0)
    one = jnp.where(row == 0, 1.0, 0.0).astype(BF16)
    qa = jnp.concatenate([high, low, one], axis=0)
    steps = bq // sub

    def scores(i):
        return dot(ka[...], qa[:, i * sub : (i + 1) * sub], 1, 0)

    s = scores(0)
    for i in range(steps):
        later = scores(i + 1) if i + 1 < steps else None
        cols = slice(i * sub, (i + 1) * sub)
        top = jnp.max(s, axis=0, keepdims=True)
        p = jnp.exp2(s - top).astype(BF16)
        o = dot(va[...], p, 1, 0)
        total = o[HEAD_DIM : HEAD_DIM + 1]
        o_ref[:, cols] = (o[:HEAD_DIM] * (1.0 / total)).astype(BF16)
        l_ref[0, :, cols] = jnp.broadcast_to(top + jnp.log2(total), (8, sub))
        s = later


def attend_call(q, k, v, bias):
    f, S = q.shape
    heads = f // HEAD_DIM
    bq = S
    sub = min(256, S)
    whole = pl.BlockSpec((HEAD_DIM, S), lambda h, i: (h, 0))
    block = pl.BlockSpec((HEAD_DIM, bq), lambda h, i: (h, i))
    return call(
        functools.partial(attend_kernel, sub=sub),
        "attend",
        (shape((f, S), BF16), shape((heads, 8, S), F32)),
        grid=(heads, S // bq),
        in_specs=[block, whole, whole, pl.BlockSpec((16, S), lambda h, i: (0, 0))],
        out_specs=(block, pl.BlockSpec((1, 8, bq), lambda h, i: (h, 0, i))),
        scratch_shapes=[
            pltpu.VMEM((S, 2 * HEAD_DIM + 16), BF16),
            pltpu.VMEM((HEAD_DIM + 16, S), BF16),
        ],
        flops=16 * f * S * S,
        moved=10 * f * S,
    )(q, k, v, bias)


def attend_back_kernel(
    q_ref, k_ref, v_ref, b_ref, o_ref, l_ref, g_ref, c_ref, s_ref, ck_ref, sk_ref,
    dq_ref, dk_ref, dv_ref, ka, va, dka, dva, *, sub
):
    S = k_ref.shape[1]
    bq = q_ref.shape[1]

    @pl.when(pl.program_id(1) == 0)
    def _():
        k = k_ref[...]
        one = jnp.ones((16, S), BF16)
        ka[...] = jnp.concatenate([k, k, b_ref[...], one], axis=0).T
        va[...] = jnp.concatenate([v_ref[...], one], axis=0).T
        dka[...] = jnp.zeros_like(dka)
        dva[...] = jnp.zeros_like(dva)

    q = q_ref[...].astype(F32) * SCALE
    qs = q.astype(BF16)
    high, low = split(q * LOG2E, 2)
    row = lax.broadcasted_iota(jnp.int32, (16, bq), 0)

    def spread(x):
        a, b, c = [y.astype(F32) for y in split(x, 3)]
        rest = jnp.where(row == 2, c, 0.0)
        return jnp.where(row == 0, a, jnp.where(row == 1, b, rest)).astype(BF16)

    one = jnp.where(row == 0, 1.0, 0.0).astype(BF16)
    g = g_ref[...]
    qa = jnp.concatenate([high, low, one, spread(-l_ref[0, 0:1])], axis=0)
    centre = jnp.sum(g.astype(F32) * o_ref[...].astype(F32), axis=0, keepdims=True)
    ga = jnp.concatenate([g, spread(-centre)], axis=0)
    for i in range(bq // sub):
        cols = slice(i * sub, (i + 1) * sub)
        p = jnp.exp2(dot(ka[...], qa[:, cols], 1, 0))
        p_low = p.astype(BF16)
        ds = (p * dot(va[...], ga[:, cols], 1, 0)).astype(BF16)
        dva[...] += dot(g[:, cols], p_low, 1, 1)
        dka[...] += dot(qs[:, cols], ds, 1, 1)
        dq = dot(k_ref[...], ds, 1, 0) * SCALE
        dq_ref[:, cols] = turn_back(dq, c_ref[:, cols], s_ref[:, cols]).astype(BF16)

    @pl.when(pl.program_id(1) == pl.num_programs(1) - 1)
    def _():
        dk_ref[...] = turn_back(dka[...], ck_ref[...], sk_ref[...]).astype(BF16)
        dv_ref[...] = dva[...].astype(BF16)


def attend_back_call(q, k, v, bias, o, lse, g, cos, sin):
    f, S = q.shape
    heads = f // HEAD_DIM
    bq = min(1024, S)
    half = HEAD_DIM // 2
    whole = pl.BlockSpec((HEAD_DIM, S), lambda h, i: (h, 0))
    block = pl.BlockSpec((HEAD_DIM, bq), lambda h, i: (h, i))
    table = pl.BlockSpec((half, S), lambda h, i: (0, 0))
    table_block = pl.BlockSpec((half, bq), lambda h, i: (0, i))
    return call(
        functools.partial(attend_back_kernel, sub=min(256, S)),
        "attend_back",
        (shape((f, S), BF16),) * 3,
        grid=(heads, S // bq),
        in_specs=[
            block, whole, whole,
            pl.BlockSpec((16, S), lambda h, i: (0, 0)),
            block,
            pl.BlockSpec((1, 8, bq), lambda h, i: (h, 0, i)),
            block, table_block, table_block, table, table,
        ],
        out_specs=(block, whole, whole),
        scratch_shapes=[
            pltpu.VMEM((S, 2 * HEAD_DIM + 32), BF16),
            pltpu.VMEM((S, HEAD_DIM + 16), BF16),
            pltpu.VMEM((HEAD_DIM, S), F32),
            pltpu.VMEM((HEAD_DIM, S), F32),
        ],
        flops=40 * f * S * S,
        moved=20 * f * S,
    )(q, k, v, bias, o, lse, g, cos, sin, cos, sin)


def out_kernel(n_parts, o_ref, w_ref, *outs):
    n = outs[0].shape[0]
    for i, out in enumerate(outs):
        out[...] = dot(o_ref[:, i * n : (i + 1) * n], w_ref[...], 0, 0).astype(BF16)


def out_call(o, w, n_parts):
    f, S = o.shape
    d = w.shape[1]
    return call(
        functools.partial(out_kernel, n_parts),
        "output_projection",
        (shape((S // n_parts, d), BF16),) * n_parts,
        flops=2 * f * S * d,
        moved=2 * (f * S + f * d + S * d),
    )(o, w)


def heads_grad_kernel(n_parts, o_ref, w_ref, *refs):
    parts, (g_ref, dw_ref) = refs[:n_parts], refs[n_parts:]
    n = parts[0].shape[0]
    total = None
    for i, p in enumerate(parts):
        cols = slice(i * n, (i + 1) * n)
        g_ref[:, cols] = dot(w_ref[...], p[...], 1, 1).astype(BF16)
        term = dot(o_ref[:, cols], p[...], 1, 0)
        total = term if total is None else total + term
    dw_ref[...] = total.astype(BF16)


def heads_grad_call(o, w, parts):
    f, S = o.shape
    d = w.shape[1]
    return call(
        functools.partial(heads_grad_kernel, len(parts)),
        "heads_grad",
        (shape((f, S), BF16), shape((f, d), BF16)),
        flops=4 * f * S * d,
        moved=2 * (2 * f * S + 2 * f * d + S * d),
    )(o, w, *parts)


def qkv_back_kernel(n_parts, w_ref, q_ref, k_ref, v_ref, *refs):
    parts, outs, dw_ref = refs[:n_parts], refs[n_parts : 2 * n_parts], refs[-1]
    n = parts[0].shape[0]
    grads = (q_ref, k_ref, v_ref)
    for i, out in enumerate(outs):
        cols = slice(i * n, (i + 1) * n)
        total = dot(grads[0][:, cols], w_ref[0], 0, 1)
        for j in (1, 2):
            total = total + dot(grads[j][:, cols], w_ref[j], 0, 1)
        out[...] = total.astype(BF16)
    for j in range(3):
        total = dot(parts[0][...], grads[j][:, 0:n], 0, 1)
        for i in range(1, n_parts):
            total = total + dot(parts[i][...], grads[j][:, i * n : (i + 1) * n], 0, 1)
        dw_ref[j] = total.astype(BF16)


def qkv_back_call(w, dq, dk, dv, parts):
    f, S = dq.shape
    n, d = parts[0].shape
    res = call(
        functools.partial(qkv_back_kernel, len(parts)),
        "qkv_back",
        tuple([shape((n, d), BF16)] * len(parts) + [shape((3, d, f), BF16)]),
        flops=12 * f * S * d,
        moved=2 * (3 * f * S + 6 * f * d + 2 * S * d),
    )(w, dq, dk, dv, *parts)
    return res[:-1], res[-1]


def ffn_kernel(groups, *refs):
    x_ref, c_ref = refs[:2]
    weights = refs[2 : 2 + 3 * groups]
    h_ref, gl_ref, ul_ref, out_ref, dx_ref = refs[2 + 3 * groups :]
    x, c = x_ref[...], c_ref[...]
    out = dx = None
    for m in range(groups):
        wg, wu, wd = [r[...].reshape(-1, r.shape[-1]) for r in weights[3 * m : 3 * m + 3]]
        gate = dot(x, wg, 1, 1)
        up = dot(x, wu, 1, 1)
        hg = dot(c, wd, 1, 1)
        sig = jax.nn.sigmoid(gate)
        act = gate * sig
        hidden = (act * up).astype(BF16)
        gl = (hg * up * (sig * (1.0 + gate * (1.0 - sig)))).astype(BF16)
        ul = (hg * act).astype(BF16)
        cols = slice(m * wg.shape[0], (m + 1) * wg.shape[0])
        h_ref[:, cols] = hidden
        gl_ref[:, cols] = gl
        ul_ref[:, cols] = ul
        o = dot(hidden, wd, 1, 0)
        e = dot(gl, wg, 1, 0) + dot(ul, wu, 1, 0)
        out = o if out is None else out + o
        dx = e if dx is None else dx + e
    out_ref[...] = out.astype(BF16)
    dx_ref[...] = dx.astype(BF16)


def ffn_call(x, c, weights):
    n, d = x.shape
    groups = len(weights)
    T, _, us, _ = weights[0].shape
    units = groups * T * us
    b = min(256, n)
    row = pl.BlockSpec((b, d), lambda i: (i, 0))
    urow = pl.BlockSpec((b, units), lambda i: (i, 0))
    specs, args = [], []
    for w in weights:
        for j in range(3):
            specs.append(
                pl.BlockSpec((T, None, us, d), functools.partial(lambda j, i: (0, j, 0, 0), j))
            )
            args.append(w)
    return call(
        functools.partial(ffn_kernel, groups),
        "feed_forward",
        (shape((n, units), BF16),) * 3 + (shape((n, d), BF16),) * 2,
        grid=(n // b,),
        in_specs=[row, row] + specs,
        out_specs=(urow,) * 3 + (row, row),
        flops=12 * n * d * units,
        moved=2 * (4 * n * d + 3 * n * units + 3 * d * units),
    )(x, c, *args)


def ffn_weight_kernel(n_parts, T, us, *refs):
    x, c, h, gl, ul = [refs[i * n_parts : (i + 1) * n_parts] for i in range(5)]
    dn_ref, gu_ref = refs[5 * n_parts :]

    def product(a, b):
        total = dot(a[0][...], b[0][...], 0, 0)
        for i in range(1, n_parts):
            total = total + dot(a[i][...], b[i][...], 0, 0)
        return total.astype(BF16)

    dn_ref[...] = product(h, c).reshape(dn_ref.shape)
    for j, g in enumerate((gl, ul)):
        dw = product(x, g)
        for t in range(dn_ref.shape[0]):
            gu_ref[t, j] = dw[:, t * us : (t + 1) * us]


def ffn_weight_call(x, c, h, gl, ul, m, T, us):
    n_parts = len(x)
    n, d = x[0].shape
    tb = max(1, min(T, 256 // us))
    row = pl.BlockSpec((n, d), lambda i: (0, 0))
    urow = pl.BlockSpec((n, tb * us), lambda i: (0, m * (T // tb) + i))
    return call(
        functools.partial(ffn_weight_kernel, n_parts, T, us),
        "feed_forward_weights",
        (shape((T, us, d), BF16), shape((T, 2, d, us), BF16)),
        grid=(T // tb,),
        in_specs=[row] * (2 * n_parts) + [urow] * (3 * n_parts),
        out_specs=(
            pl.BlockSpec((tb, us, d), lambda i: (i, 0, 0)),
            pl.BlockSpec((tb, 2, d, us), lambda i: (i, 0, 0, 0)),
        ),
        flops=6 * n * n_parts * d * T * us,
        moved=2 * (2 * n * n_parts * d + 3 * n * n_parts * T * us + 3 * d * T * us),
    )(*x, *c, *h, *gl, *ul)


def build(DP, T):
    M = DP // 4
    R = T // 2

    def parts_of(d):
        return d // (DP // 2), (d // 2) % M, d % 2

    def over_dp(x, f):
        return lax.ppermute(x, "dp", [(i, f(i)) for i in range(DP)])

    def core_flip(x):
        return over_dp(x, lambda i: i ^ 1)

    def top_flip(x):
        return over_dp(x, lambda i: (i + DP // 2) % DP)

    def mid_from(x, k):
        def dest(i):
            a, m, c = parts_of(i)
            return a * (DP // 2) + ((m - k) % M) * 2 + c

        return over_dp(x, dest)

    def row_from(x, k):
        return lax.ppermute(
            x, "tensor", [((t // R) * R + (t % R + k) % R, t) for t in range(T)]
        )

    def half_swap(x):
        return lax.ppermute(x, "tensor", [(t, (t + R) % T) for t in range(T)])

    def reshard(x):
        pairs = []
        for d in range(DP):
            for t in range(T):
                j, c, h, r = d // 2, d % 2, t // R, t % R
                pairs.append((d * T + t, (2 * j + h) * T + c * R + r))
        return lax.ppermute(x, ("dp", "tensor"), pairs)

    def gather_heads(x):
        out = []
        for k in range(R):
            y = x if k == 0 else row_from(x, k)
            out += [y, core_flip(y)]
        return out

    def scatter_heads(pieces):
        out = []
        for k in range(R):
            mine, theirs = pieces[2 * k], core_flip(pieces[2 * k + 1])
            if k == 0:
                out += [mine, theirs]
            else:
                both = (mine.astype(F32) + theirs.astype(F32)).astype(BF16)
                out.append(row_from(both, R - k))
        return out

    def on_device(
        tokens, qkv_weight, output_projection_weight, gate_up_weight, down_projection_weight,
        attention_gain, feedforward_gain, window_lengths, key_mask, cotangent,
    ):
        n, _, d = tokens.shape
        length = key_mask.shape[0]
        me_d, me_t = lax.axis_index("dp"), lax.axis_index("tensor")
        core, h, r = me_d % 2, me_t // R, me_t % R
        us = down_projection_weight.shape[0] // DP
        gain_one, gain_two = attention_gain[None], feedforward_gain[None]

        x = reshard(tokens[:, 0])
        wq_own = qkv_weight.transpose(1, 0, 2)
        f = wq_own.shape[2]
        flat = wq_own.reshape(3 * d, f)
        wq_far = lax.all_gather(
            half_swap(lax.dynamic_slice_in_dim(flat, me_d * (3 * d // DP), 3 * d // DP, 0)),
            "dp", axis=0, tiled=True,
        ).reshape(3, d, f)
        fo = output_projection_weight.shape[0]
        wo_far = lax.all_gather(
            half_swap(
                lax.dynamic_slice_in_dim(output_projection_weight, me_d * (fo // DP), fo // DP, 0)
            ),
            "dp", axis=0, tiled=True,
        )
        wq = jnp.where(core == 0, wq_own, wq_far)
        wo = jnp.where(core == 0, output_projection_weight, wo_far)

        positions = jnp.arange(length, dtype=jnp.int32)
        valid = (positions < window_lengths[0]) & (key_mask[:, 0] == 1)
        bias_own = jnp.where(valid, 0.0, MASKED).astype(F32)
        bias = jnp.where(core == h, bias_own, core_flip(bias_own))
        order = jnp.stack(
            [((core + dc) % 2) * R + (r + dr) % R for dr in range(R) for dc in (0, 1)]
        )
        bias = jnp.take(bias.reshape(T, n), order, axis=0).reshape(length)
        bias = jnp.concatenate(
            [bias[None].astype(BF16), jnp.zeros((15, length), BF16)], axis=0
        )
        places = (order[:, None] * n + jnp.arange(n, dtype=jnp.int32)[None]).reshape(length)
        half = HEAD_DIM // 2
        frequencies = ROPE_BASE ** (-(jnp.arange(half, dtype=F32) * 2.0 / HEAD_DIM))
        angles = frequencies[:, None] * places.astype(F32)[None]
        cos, sin = jnp.cos(angles), jnp.sin(angles)

        normed_one = gather_heads(norm_call(x, gain_one))

        def unit_slices():
            gu = lax.dynamic_slice_in_dim(gate_up_weight, me_d * us, us, 2)
            dn = lax.dynamic_slice_in_dim(down_projection_weight, me_d * us, us, 0)
            return jnp.concatenate([gu.transpose(1, 2, 0), dn[None]], axis=0)

        slices, _ = lax.optimization_barrier((unit_slices(), normed_one[-1]))
        units = lax.all_gather(slices, "tensor", axis=0)
        weights = [units] + [mid_from(units, k) for k in range(1, M)]

        q, k, v = qkv_call(normed_one, wq, cos, sin)
        o, lse = attend_call(q, k, v, bias)
        arrived = scatter_heads(out_call(o, wo, 2 * R))
        middle, normed = middle_call(x, gain_two, arrived)

        cot = reshard(cotangent[:, 0])

        def gather_units(y):
            z = top_flip(y)
            return [y, core_flip(y), z, core_flip(z)]

        cots = gather_units(cot)
        xs = gather_units(normed)
        near = ffn_call(jnp.concatenate(xs[:2]), jnp.concatenate(cots[:2]), weights)
        far = ffn_call(jnp.concatenate(xs[2:]), jnp.concatenate(cots[2:]), weights)

        def scatter_units(i):
            def both(y):
                return y[:n], core_flip(y[n:])

            mine, theirs = both(far[i])
            crossed = top_flip((mine.astype(F32) + theirs.astype(F32)).astype(BF16))
            return [*both(near[i]), crossed]

        dx_parts = scatter_units(4)
        middle_grad, middle_low, gain_two_part = back_call(
            "middle_grad", cot, middle, gain_two, dx_parts, 1
        )

        def weight_grads(m):
            cat = [jnp.concatenate(z) for z in (xs[:2], xs[2:], cots[:2], cots[2:])]
            return ffn_weight_call(
                cat[:2], cat[2:], *[[near[i], far[i]] for i in range(3)], m, T, us
            )

        grads = None
        for m in range(M - 1, -1, -1):
            got = weight_grads(m)
            if m:
                got = [mid_from(g, M - m) for g in got]
            got = [g.astype(F32) for g in got]
            grads = got if grads is None else [a + b for a, b in zip(grads, got)]
        dn_grad, gu_grad = [
            lax.all_gather(
                lax.psum_scatter(g.astype(BF16), "tensor", scatter_dimension=0, tiled=False),
                "dp", axis=0,
            )
            for g in grads
        ]
        down_grad = dn_grad.reshape(DP * us, d).astype(F32)
        gate_up_grad = gu_grad.transpose(2, 1, 0, 3).reshape(d, 2, DP * us).astype(F32)

        output = reshard(output_call(middle, scatter_units(3)))[:, None]

        lows = gather_heads(middle_low)
        g, wo_grad = heads_grad_call(o, wo, lows)
        dq, dk, dv = attend_back_call(q, k, v, bias, o, lse, g, cos, sin)
        dx_pieces, wq_grad = qkv_back_call(wq, dq, dk, dv, normed_one)
        arrived = scatter_heads(dx_pieces)
        tokens_low, gain_one_part = back_call(
            "tokens_grad", middle_grad, x, gain_one, arrived, 0
        )
        tokens_grad = reshard(tokens_low)[:, None]

        same_core = [[i for i in range(DP) if i % 2 == c] for c in (0, 1)]

        def reduce_heads(g):
            part = lax.psum_scatter(
                g, "dp", scatter_dimension=0, tiled=True, axis_index_groups=same_core
            )
            pairs = [
                ((2 * j + 1) * T + t, 2 * j * T + (t + R) % T)
                for j in range(DP // 2)
                for t in range(T)
            ]
            part = part.astype(F32) + lax.ppermute(part, ("dp", "tensor"), pairs).astype(F32)
            part = part.astype(BF16)
            part = jnp.where(core == 0, part, core_flip(part))
            return lax.all_gather(
                part, "dp", axis=0, tiled=True, axis_index_groups=same_core
            ).astype(F32)

        qkv_grad = reduce_heads(wq_grad.reshape(3 * d, f)).reshape(3, d, f).transpose(1, 0, 2)
        out_grad = reduce_heads(wo_grad)
        gains = lax.psum(
            jnp.concatenate([gain_one_part, gain_two_part], axis=0), ("dp", "tensor")
        )
        return (
            output, tokens_grad, qkv_grad, out_grad, gate_up_grad, down_grad, gains[0], gains[1]
        )

    return on_device


def solution(mesh):
    return jax.shard_map(
        build(mesh.shape["dp"], mesh.shape["tensor"]),
        mesh=mesh,
        in_specs=(
            P("tensor", "dp", None),
            P(None, None, "tensor"),
            P("tensor", None),
            P(None, None, "tensor"),
            P("tensor", None),
            P(),
            P(),
            P("dp"),
            P(None, "dp"),
            P("tensor", "dp", None),
        ),
        out_specs=(
            P("tensor", "dp", None),
            P("tensor", "dp", None),
            P(None, None, "tensor"),
            P("tensor", None),
            P(None, None, "tensor"),
            P("tensor", None),
            P(),
            P(),
        ),
        check_vma=False,
    )
```

```python
import functools
import math

import jax
import jax.numpy as jnp
from jax import lax
from jax.experimental import pallas as pl
from jax.experimental.pallas import tpu as pltpu
from jax.sharding import PartitionSpec as P

HEAD_DIM = 64
EPSILON = 1e-05
MASKED = -1000000000.0
ROPE_BASE = 10000.0
LOG2E = math.log2(math.e)
SCALE = HEAD_DIM ** (-0.5)
BF16 = jnp.bfloat16
F32 = jnp.float32
MIB = 1 << 20
PER_US = 1.15e9 * 0.25


def dot(a, b, ca, cb):
    return lax.dot_general(a, b, (((ca,), (cb,)), ((), ())), preferred_element_type=F32)


def call(body, name, out, us, vmem=56, **kw):
    return pl.pallas_call(
        body,
        out_shape=out,
        name=name,
        compiler_params=pltpu.CompilerParams(vmem_limit_bytes=vmem * MIB),
        cost_estimate=pl.CostEstimate(
            flops=int(us * PER_US), bytes_accessed=0, transcendentals=0
        ),
        **kw,
    )


def shape(s, d):
    return jax.ShapeDtypeStruct(s, d)


def norm_rows(x, gain):
    centered = x - jnp.mean(x, axis=-1, keepdims=True)
    inverse = lax.rsqrt(jnp.mean(centered * centered, axis=-1, keepdims=True) + EPSILON)
    scaled = centered * inverse
    return scaled * gain, scaled, inverse


def norm_kernel(x_ref, g_ref, o_ref):
    o_ref[...] = norm_rows(x_ref[...].astype(F32), g_ref[...])[0].astype(BF16)


def norm_call(x, gain):
    n, d = x.shape
    b = min(128, n)
    return call(
        norm_kernel,
        "norm_tokens",
        shape((n, d), BF16),
        grid=(n // b,),
        in_specs=[pl.BlockSpec((b, d), lambda i: (i, 0)), pl.BlockSpec((1, d), lambda i: (0, 0))],
        out_specs=pl.BlockSpec((b, d), lambda i: (i, 0)),
        us=2.2,
    )(x, gain)


def middle_kernel(x_ref, g_ref, *refs):
    parts, (m_ref, o_ref) = refs[:-2], refs[-2:]
    m = x_ref[...].astype(F32)
    for p in parts:
        m = m + p[...].astype(F32)
    m_ref[...] = m
    o_ref[...] = norm_rows(m, g_ref[...])[0].astype(BF16)


def middle_call(x, gain, parts):
    n, d = x.shape
    b = min(128, n)
    row = pl.BlockSpec((b, d), lambda i: (i, 0))
    return call(
        middle_kernel,
        "middle_norm",
        (shape((n, d), F32), shape((n, d), BF16)),
        grid=(n // b,),
        in_specs=[row, pl.BlockSpec((1, d), lambda i: (0, 0))] + [row] * len(parts),
        out_specs=(row, row),
        us=4.5,
    )(x, gain, *parts)


def back_kernel(n_parts, keep, base_ref, x_ref, g_ref, *refs):
    parts, outs = refs[:n_parts], refs[n_parts:]
    e = parts[0][...].astype(F32)
    for p in parts[1:]:
        e = e + p[...].astype(F32)
    gain = g_ref[...]
    _, scaled, inverse = norm_rows(x_ref[...].astype(F32), gain)
    through = e * gain
    first = jnp.mean(through, axis=-1, keepdims=True)
    second = jnp.mean(through * scaled, axis=-1, keepdims=True)
    total = base_ref[...].astype(F32) + inverse * (through - first - scaled * second)
    if keep:
        outs[0][...] = total
    outs[-2][...] = total.astype(BF16)

    @pl.when(pl.program_id(0) == 0)
    def _():
        outs[-1][...] = jnp.zeros_like(outs[-1])

    outs[-1][...] += jnp.sum(e * scaled, axis=0, keepdims=True)


def back_call(name, base, x, gain, parts, keep):
    n, d = x.shape
    b = min(128, n)
    row = pl.BlockSpec((b, d), lambda i: (i, 0))
    one = pl.BlockSpec((1, d), lambda i: (0, 0))
    out = [shape((n, d), F32)] * keep + [shape((n, d), BF16), shape((1, d), F32)]
    return call(
        functools.partial(back_kernel, len(parts), keep),
        name,
        tuple(out),
        grid=(n // b,),
        in_specs=[row, row, one] + [row] * len(parts),
        out_specs=tuple([row] * (keep + 1) + [one]),
        us=5.5,
    )(base, x, gain, *parts)


def output_kernel(m_ref, *refs):
    total = m_ref[...]
    for p in refs[:-1]:
        total = total + p[...].astype(F32)
    refs[-1][...] = total.astype(BF16)


def output_call(m, parts):
    n, d = m.shape
    b = min(256, n)
    row = pl.BlockSpec((b, d), lambda i: (i, 0))
    return call(
        output_kernel,
        "output_sum",
        shape((n, d), BF16),
        grid=(n // b,),
        in_specs=[row] * (1 + len(parts)),
        out_specs=row,
        us=3.6,
    )(m, *parts)


def turn(u, cos, sin):
    half = HEAD_DIM // 2
    first, second = u[:half], u[half:]
    return jnp.concatenate([first * cos - second * sin, second * cos + first * sin], axis=0)


def turn_back(u, cos, sin):
    half = HEAD_DIM // 2
    first, second = u[:half], u[half:]
    return jnp.concatenate([first * cos + second * sin, second * cos - first * sin], axis=0)


def part_cols(i, n_parts, n):
    at = (i % (n_parts // 2)) * 2 + i // (n_parts // 2)
    return slice(at * n, (at + 1) * n)


def qkv_kernel(n_parts, c_ref, s_ref, w_ref, *refs):
    parts, (q_ref, k_ref, v_ref) = refs[:n_parts], refs[n_parts:]
    n, d = parts[0].shape
    f = w_ref.shape[-1]
    for which, out in enumerate((q_ref, k_ref, v_ref)):
        w = w_ref[:, which].reshape(d, f)
        for i, p in enumerate(parts):
            cols = part_cols(i, n_parts, n)
            cos, sin = c_ref[:, cols], s_ref[:, cols]
            u = dot(w, p[...], 0, 1)
            for h in range(f // HEAD_DIM):
                rows = slice(h * HEAD_DIM, (h + 1) * HEAD_DIM)
                head = u[rows]
                if which < 2:
                    head = turn(head, cos, sin)
                out[rows, cols] = head.astype(BF16)


def qkv_call(parts, pack, cos, sin):
    n, d = parts[0].shape
    f = pack.shape[-1]
    total = n * len(parts)
    return call(
        functools.partial(qkv_kernel, len(parts)),
        "project_heads",
        (shape((f, total), BF16),) * 3,
        us=7.6,
    )(cos, sin, pack, *parts)


def split(x, n):
    out = []
    for _ in range(n):
        h = x.astype(BF16)
        out.append(h)
        x = x - h.astype(F32)
    return out


def attend_kernel(q_ref, k_ref, v_ref, b_ref, o_ref, l_ref, ka, va, *, sub):
    S = k_ref.shape[1]
    bq = q_ref.shape[1]

    @pl.when(pl.program_id(1) == 0)
    def _():
        k = k_ref[...]
        ka[...] = jnp.concatenate([k, k, b_ref[...]], axis=0).T
        va[0:HEAD_DIM] = v_ref[...]
        va[HEAD_DIM:] = jnp.ones((16, S), BF16)

    high, low = split(q_ref[...].astype(F32) * (SCALE * LOG2E), 2)
    row = lax.broadcasted_iota(jnp.int32, (16, bq), 0)
    one = jnp.where(row == 0, 1.0, 0.0).astype(BF16)
    qa = jnp.concatenate([high, low, one], axis=0)
    steps = bq // sub

    def scores(i):
        return dot(ka[...], qa[:, i * sub : (i + 1) * sub], 1, 0)

    s = scores(0)
    for i in range(steps):
        later = scores(i + 1) if i + 1 < steps else None
        cols = slice(i * sub, (i + 1) * sub)
        top = jnp.max(s, axis=0, keepdims=True)
        p = jnp.exp2(s - top).astype(BF16)
        o = dot(va[...], p, 1, 0)
        total = o[HEAD_DIM : HEAD_DIM + 1]
        o_ref[:, cols] = (o[:HEAD_DIM] * (1.0 / total)).astype(BF16)
        l_ref[0, :, cols] = jnp.broadcast_to(top + jnp.log2(total), (8, sub))
        s = later


def attend_call(q, k, v, bias, first, count):
    S = q.shape[1]
    bq = S
    sub = min(256, S)
    whole = pl.BlockSpec((HEAD_DIM, S), lambda h, i: (h + first, 0))
    block = pl.BlockSpec((HEAD_DIM, bq), lambda h, i: (h + first, i))
    return call(
        functools.partial(attend_kernel, sub=sub),
        "attend",
        (shape((count * HEAD_DIM, S), BF16), shape((count, 8, S), F32)),
        grid=(count, S // bq),
        in_specs=[block, whole, whole, pl.BlockSpec((16, S), lambda h, i: (0, 0))],
        out_specs=(
            pl.BlockSpec((HEAD_DIM, bq), lambda h, i: (h, i)),
            pl.BlockSpec((1, 8, bq), lambda h, i: (h, 0, i)),
        ),
        scratch_shapes=[
            pltpu.VMEM((S, 2 * HEAD_DIM + 16), BF16),
            pltpu.VMEM((HEAD_DIM + 16, S), BF16),
        ],
        us=7.4 * count,
    )(q, k, v, bias)


def attend_back_kernel(
    q_ref, k_ref, v_ref, b_ref, o_ref, l_ref, g_ref, c_ref, s_ref, ck_ref, sk_ref,
    dq_ref, dk_ref, dv_ref, ka, va, dka, dva, *, sub
):
    S = k_ref.shape[1]
    bq = q_ref.shape[1]

    @pl.when(pl.program_id(1) == 0)
    def _():
        k = k_ref[...]
        one = jnp.ones((16, S), BF16)
        ka[...] = jnp.concatenate([k, k, b_ref[...], one], axis=0).T
        va[...] = jnp.concatenate([v_ref[...], one], axis=0).T
        dka[...] = jnp.zeros_like(dka)
        dva[...] = jnp.zeros_like(dva)

    q = q_ref[...].astype(F32) * SCALE
    qs = q.astype(BF16)
    high, low = split(q * LOG2E, 2)
    row = lax.broadcasted_iota(jnp.int32, (16, bq), 0)

    def spread(x):
        a, b, c = [y.astype(F32) for y in split(x, 3)]
        rest = jnp.where(row == 2, c, 0.0)
        return jnp.where(row == 0, a, jnp.where(row == 1, b, rest)).astype(BF16)

    one = jnp.where(row == 0, 1.0, 0.0).astype(BF16)
    g = g_ref[...]
    qa = jnp.concatenate([high, low, one, spread(-l_ref[0, 0:1])], axis=0)
    centre = jnp.sum(g.astype(F32) * o_ref[...].astype(F32), axis=0, keepdims=True)
    ga = jnp.concatenate([g, spread(-centre)], axis=0)
    for i in range(bq // sub):
        cols = slice(i * sub, (i + 1) * sub)
        p = jnp.exp2(dot(ka[...], qa[:, cols], 1, 0))
        p_low = p.astype(BF16)
        ds = (p * dot(va[...], ga[:, cols], 1, 0)).astype(BF16)
        dva[...] += dot(g[:, cols], p_low, 1, 1)
        dka[...] += dot(qs[:, cols], ds, 1, 1)
        dq = dot(k_ref[...], ds, 1, 0) * SCALE
        dq_ref[:, cols] = turn_back(dq, c_ref[:, cols], s_ref[:, cols]).astype(BF16)

    @pl.when(pl.program_id(1) == pl.num_programs(1) - 1)
    def _():
        dk_ref[...] = turn_back(dka[...], ck_ref[...], sk_ref[...]).astype(BF16)
        dv_ref[...] = dva[...].astype(BF16)


def attend_back_call(q, k, v, bias, o, lse, g, cos, sin, head, place):
    S = q.shape[1]
    bq = min(1024, S)
    half = HEAD_DIM // 2
    whole = pl.BlockSpec((HEAD_DIM, S), lambda h, i: (head, 0))
    block = pl.BlockSpec((HEAD_DIM, bq), lambda h, i: (head, i))
    table = pl.BlockSpec((half, S), lambda h, i: (0, 0))
    table_block = pl.BlockSpec((half, bq), lambda h, i: (0, i))
    return call(
        functools.partial(attend_back_kernel, sub=min(256, S)),
        "attend_back",
        (shape((HEAD_DIM, S), BF16),) * 3,
        us=12.3,
        grid=(1, S // bq),
        in_specs=[
            block, whole, whole,
            pl.BlockSpec((16, S), lambda h, i: (0, 0)),
            pl.BlockSpec((HEAD_DIM, bq), lambda h, i: (place, i)),
            pl.BlockSpec((1, 8, bq), lambda h, i: (place, 0, i)),
            block, table_block, table_block, table, table,
        ],
        out_specs=(
            pl.BlockSpec((HEAD_DIM, bq), lambda h, i: (0, i)),
            pl.BlockSpec((HEAD_DIM, S), lambda h, i: (0, 0)),
            pl.BlockSpec((HEAD_DIM, S), lambda h, i: (0, 0)),
        ),
        scratch_shapes=[
            pltpu.VMEM((S, 2 * HEAD_DIM + 32), BF16),
            pltpu.VMEM((S, HEAD_DIM + 16), BF16),
            pltpu.VMEM((HEAD_DIM, S), F32),
            pltpu.VMEM((HEAD_DIM, S), F32),
        ],
    )(q, k, v, bias, o, lse, g, cos, sin, cos, sin)


def stack_rows(refs, cols):
    return jnp.concatenate([r[:, cols] for r in refs], axis=0)


def out_kernel(n_heads, w_ref, *refs):
    heads, outs = refs[:n_heads], refs[n_heads:]
    n, d = outs[0].shape
    J, b = w_ref.shape[0], w_ref.shape[-1]
    for i, out in enumerate(outs):
        o = stack_rows(heads, slice(i * n, (i + 1) * n))
        for j in range(J):
            out[:, j * b : (j + 1) * b] = dot(o, w_ref[j], 0, 0).astype(BF16)


def pack_spec(pack, which):
    J, _, a, b = pack.shape
    return pl.BlockSpec((J, None, a, b), lambda i: (0, which, 0, 0))


def full(s):
    return pl.BlockSpec(s, lambda i: (0,) * len(s))


def out_call(heads, pack, n_parts, d):
    S = heads[0].shape[1]
    f = sum(o.shape[0] for o in heads)
    return call(
        functools.partial(out_kernel, len(heads)),
        "output_projection",
        (shape((S // n_parts, d), BF16),) * n_parts,
        grid=(1,),
        in_specs=[pack_spec(pack, 3)] + [full(o.shape) for o in heads],
        out_specs=(full((S // n_parts, d)),) * n_parts,
        us=4.2,
    )(pack, *heads)


def heads_grad_kernel(n_heads, n_parts, w_ref, *refs):
    heads, parts, (g_ref, dw_ref) = (
        refs[:n_heads], refs[n_heads : n_heads + n_parts], refs[n_heads + n_parts :]
    )
    n = parts[0].shape[0]
    J, b = w_ref.shape[0], w_ref.shape[-1]
    w = jnp.concatenate([w_ref[j] for j in range(J)], axis=1)
    total = None
    for i, p in enumerate(parts):
        cols = slice(i * n, (i + 1) * n)
        g_ref[:, cols] = dot(w, p[...], 1, 1).astype(BF16)
        term = dot(stack_rows(heads, cols), p[...], 1, 0)
        total = term if total is None else total + term
    for j in range(J):
        dw_ref[j] = total[:, j * b : (j + 1) * b].astype(BF16)


def heads_grad_call(heads, pack, parts):
    S = heads[0].shape[1]
    f = sum(o.shape[0] for o in heads)
    n, d = parts[0].shape
    J, _, a, b = pack.shape
    return call(
        functools.partial(heads_grad_kernel, len(heads), len(parts)),
        "heads_grad",
        (shape((f, S), BF16), shape((J, a, b), BF16)),
        grid=(1,),
        in_specs=[pack_spec(pack, 3)] + [full(o.shape) for o in heads] + [full((n, d))] * len(parts),
        out_specs=(full((f, S)), full((J, a, b))),
        us=6,
    )(pack, *heads, *parts)


def qkv_back_kernel(n_parts, n_groups, w_ref, *refs):
    grads, outs = refs[: 3 * n_groups], refs[3 * n_groups :]
    n, d = outs[0].shape
    f = w_ref.shape[-1]
    for i, out in enumerate(outs):
        cols = slice(i * n, (i + 1) * n)
        total = None
        for j in range(3):
            g = stack_rows(grads[j::3], cols)
            term = dot(g, w_ref[:, j].reshape(d, f), 0, 1)
            total = term if total is None else total + term
        out[...] = total.astype(BF16)


def qkv_back_call(pack, grads, n_parts, d):
    f = pack.shape[-1]
    S = grads[0][0].shape[1]
    flat = [g for group in grads for g in group]
    return call(
        functools.partial(qkv_back_kernel, n_parts, len(grads)),
        "qkv_back",
        (shape((S // n_parts, d), BF16),) * n_parts,
        us=7,
    )(pack, *flat)


def qkv_weight_kernel(n_parts, n_groups, wo_ref, *refs):
    grads, parts, dw_ref = refs[: 3 * n_groups], refs[3 * n_groups : -1], refs[-1]
    n = parts[0].shape[0]
    J, _, a, b = dw_ref.shape
    for j in range(3):
        total = None
        for i, p in enumerate(parts):
            g = stack_rows(grads[j::3], part_cols(i, n_parts, n))
            term = dot(p[...], g, 0, 1)
            total = term if total is None else total + term
        dw_ref[:, j] = total.astype(BF16).reshape(J, a, b)
    dw_ref[:, 3] = wo_ref[...]


def qkv_weight_call(wo_grad, grads, parts, pack_shape):
    n, d = parts[0].shape
    f = pack_shape[-1]
    S = n * len(parts)
    flat = [g for group in grads for g in group]
    return call(
        functools.partial(qkv_weight_kernel, len(parts), len(grads)),
        "qkv_weights",
        shape(pack_shape, BF16),
        us=8,
    )(wo_grad, *flat, *parts)


def pack_kernel(n_parts, index_ref, q_ref, o_ref, *refs):
    parts, out = refs[:-1], refs[-1]
    J, _, a, b = out.shape

    @pl.when(index_ref[n_parts] == 0)
    def _():
        for j in range(J):
            for which in range(3):
                out[j, which] = q_ref[which, j * a : (j + 1) * a]
            out[j, 3] = o_ref[:, j * b : (j + 1) * b]

    @pl.when(index_ref[n_parts] == 1)
    def _():
        for i, p in enumerate(parts):
            out[index_ref[i]] = p[...]


def pack_call(index, wq, wo, parts):
    _, a, b = parts[0].shape
    J = len(parts)
    vmem = pl.BlockSpec(memory_space=pltpu.VMEM)
    return call(
        functools.partial(pack_kernel, J),
        "pack_heads",
        shape((J, 4, a, b), BF16),
        in_specs=[pl.BlockSpec(memory_space=pltpu.SMEM)] + [vmem] * (J + 2),
        out_specs=vmem,
        us=3.7,
    )(index, wq, wo, *parts)


def unpack_kernel(n_parts, index_ref, *refs):
    parts, (q_ref, o_ref) = refs[:n_parts], refs[n_parts:]
    a, b = parts[0].shape[1:]
    for i, p in enumerate(parts):
        j = index_ref[i]
        for which in range(3):
            q_ref[which, pl.ds(pl.multiple_of(j * a, a), a), :] = p[which].astype(F32)
        o_ref[:, pl.ds(pl.multiple_of(j * b, b), b)] = p[3].astype(F32)


def unpack_call(index, parts):
    _, a, b = parts[0].shape
    J = len(parts)
    vmem = pl.BlockSpec(memory_space=pltpu.VMEM)
    return call(
        functools.partial(unpack_kernel, J),
        "unpack_heads",
        (shape((3, J * a, b), F32), shape((a, J * b), F32)),
        in_specs=[pl.BlockSpec(memory_space=pltpu.SMEM)] + [vmem] * J,
        out_specs=(vmem, vmem),
        us=3.8,
    )(index, *parts)


def ffn_kernel(groups, steps, *refs):
    x0, x1, c0, c1 = refs[:4]
    weights = refs[4 : 4 + 3 * groups]
    h_ref, gl_ref, ul_ref, out0, out1, dx0, dx1 = refs[4 + 3 * groups :]
    early = pl.program_id(0) < steps
    x = jnp.where(early, x0[...], x1[...])
    c = jnp.where(early, c0[...], c1[...])
    out = dx = None
    for m in range(groups):
        wg, wu, wd = [r[...].reshape(-1, r.shape[-1]) for r in weights[3 * m : 3 * m + 3]]
        gate = dot(x, wg, 1, 1)
        up = dot(x, wu, 1, 1)
        hg = dot(c, wd, 1, 1)
        sig = jax.nn.sigmoid(gate)
        act = gate * sig
        hidden = (act * up).astype(BF16)
        gl = (hg * up * (sig * (1.0 + gate * (1.0 - sig)))).astype(BF16)
        ul = (hg * act).astype(BF16)
        cols = slice(m * wg.shape[0], (m + 1) * wg.shape[0])
        h_ref[:, cols] = hidden
        gl_ref[:, cols] = gl
        ul_ref[:, cols] = ul
        o = dot(hidden, wd, 1, 0)
        e = dot(gl, wg, 1, 0) + dot(ul, wu, 1, 0)
        out = o if out is None else out + o
        dx = e if dx is None else dx + e

    @pl.when(early)
    def _():
        out0[...] = out.astype(BF16)
        dx0[...] = dx.astype(BF16)

    @pl.when(jnp.logical_not(early))
    def _():
        out1[...] = out.astype(BF16)
        dx1[...] = dx.astype(BF16)


def ffn_call(xs, cs, weights):
    n, d = xs[0].shape
    groups = len(weights)
    T, us, _ = weights[0][0].shape
    units = groups * T * us
    b = min(256, n)
    steps = n // b
    first = pl.BlockSpec((b, d), lambda i: (jnp.minimum(i, steps - 1), 0))
    second = pl.BlockSpec((b, d), lambda i: (jnp.maximum(i - steps, 0), 0))
    urow = pl.BlockSpec((b, units), lambda i: (i, 0))
    specs, args = [], []
    for group in weights:
        specs += [pl.BlockSpec((T, us, d), lambda i: (0, 0, 0))] * 3
        args += group
    return call(
        functools.partial(ffn_kernel, groups, steps),
        "feed_forward",
        (shape((2 * n, units), BF16),) * 3 + (shape((n, d), BF16),) * 4,
        grid=(2 * steps,),
        in_specs=[first, second, first, second] + specs,
        out_specs=(urow,) * 3 + (first, second, first, second),
        us=21,
    )(*xs, *cs, *args)


def ffn_weight_kernel(T, us, *refs):
    x, c = refs[:4], refs[4:8]
    h, gl, ul = refs[8:10], refs[10:12], refs[12:14]
    outs = refs[14:]
    n = x[0].shape[0]

    def product(a, b):
        total = None
        for i in range(4):
            rows = slice((i % 2) * n, (i % 2 + 1) * n)
            term = dot(a[i][...], b(i, rows), 0, 0)
            total = term if total is None else total + term
        return total.astype(BF16)

    dw = product(c, lambda i, rows: h[i // 2][rows])
    for t in range(T):
        outs[1][t, 1] = dw[:, t * us : (t + 1) * us]
    dw = product(x, lambda i, rows: jnp.concatenate([gl[i // 2][rows], ul[i // 2][rows]], axis=1))
    for t in range(T):
        outs[0][t] = dw[:, t * us : (t + 1) * us]
        outs[1][t, 0] = dw[:, (T + t) * us : (T + t + 1) * us]


def ffn_weight_call(x, c, h, gl, ul, m, T, us):
    n, d = x[0].shape
    db = min(256, d)
    spec = [pl.BlockSpec((n, db), lambda i: (0, i))] * 8
    spec += [pl.BlockSpec((2 * n, T * us), lambda i: (0, m))] * 6
    return call(
        functools.partial(ffn_weight_kernel, T, us),
        "feed_forward_weights",
        (shape((T, d, us), BF16), shape((T, 2, d, us), BF16)),
        grid=(d // db,),
        in_specs=spec,
        out_specs=(
            pl.BlockSpec((T, db, us), lambda i: (0, i, 0)),
            pl.BlockSpec((T, 2, db, us), lambda i: (0, 0, i, 0)),
        ),
        us=12.4,
    )(*x, *c, *h, *gl, *ul)


def assemble_kernel(w_ref, gu_ref, dn_ref):
    DP, _, _, us = w_ref.shape
    for j in range(2):
        rows = jnp.concatenate([w_ref[p, j] for p in range(DP)], axis=1)
        gu_ref[:, j, :] = rows.astype(F32)
    rows = jnp.concatenate([w_ref[p, 2] for p in range(DP)], axis=1)
    dn_ref[...] = rows.T.astype(F32)


def assemble_call(w):
    DP, _, d, us = w.shape
    b = min(256, d)
    return call(
        assemble_kernel,
        "feed_forward_gradients",
        (shape((d, 2, DP * us), F32), shape((DP * us, d), F32)),
        grid=(d // b,),
        in_specs=[pl.BlockSpec((DP, 3, b, us), lambda i: (0, 0, i, 0))],
        out_specs=(
            pl.BlockSpec((b, 2, DP * us), lambda i: (i, 0, 0)),
            pl.BlockSpec((DP * us, b), lambda i: (0, i)),
        ),
        us=8,
    )(w)


def after(x, *deps):
    return lax.optimization_barrier((x, *deps))[0]


def tie(*xs):
    return lax.optimization_barrier(xs)


def build(DP, T):
    M = DP // 4
    R = T // 2
    J = DP // 2

    def over_dp(x, f):
        return lax.ppermute(x, "dp", [(i, f(i)) for i in range(DP)])

    def core_flip(x):
        return over_dp(x, lambda i: i ^ 1)

    def top_flip(x):
        return over_dp(x, lambda i: (i + DP // 2) % DP)

    def mid_from(x, k):
        def dest(i):
            a, m, c = i // (DP // 2), (i // 2) % M, i % 2
            return a * (DP // 2) + ((m - k) % M) * 2 + c

        return over_dp(x, dest)

    def pair_from(x, k):
        return over_dp(x, lambda i: ((i // 2) ^ k) * 2 + i % 2)

    def row_from(x, k):
        return lax.ppermute(
            x, "tensor", [((t // R) * R + (t % R + k) % R, t) for t in range(T)]
        )

    def reshard(x):
        pairs = []
        for d in range(DP):
            for t in range(T):
                j, c, h, r = d // 2, d % 2, t // R, t % R
                pairs.append((d * T + t, (2 * j + h) * T + c * R + r))
        return lax.ppermute(x, ("dp", "tensor"), pairs)

    def send_rows(x):
        return [row_from(x, k) for k in range(1, R)]

    def gather_heads(x, flipped, rows, hold):
        out = [x, flipped]
        for y in rows:
            y = after(y, hold)
            out += [y, core_flip(y)]
        return out

    def scatter_heads(pieces):
        out = []
        for k in range(R):
            mine, theirs = pieces[2 * k], core_flip(pieces[2 * k + 1])
            if k == 0:
                out += [mine, theirs]
            else:
                both = (mine.astype(F32) + theirs.astype(F32)).astype(BF16)
                out.append(row_from(both, R - k))
        return out

    def gather_units(y):
        z = top_flip(y)
        return [y, core_flip(y), z, core_flip(z)]

    def sum_all(x):
        for bit in range(DP.bit_length() - 1):
            x = x + over_dp(x, lambda i, bit=bit: i ^ (1 << bit))
        for bit in range(T.bit_length() - 1):
            x = x + lax.ppermute(x, "tensor", [(t, t ^ (1 << bit)) for t in range(T)])
        return x

    def on_device(
        tokens, qkv_weight, output_projection_weight, gate_up_weight, down_projection_weight,
        attention_gain, feedforward_gain, window_lengths, key_mask, cotangent,
    ):
        n, _, d = tokens.shape
        length = key_mask.shape[0]
        me_d, me_t = lax.axis_index("dp"), lax.axis_index("tensor")
        core, h, r, pair = me_d % 2, me_t // R, me_t % R, me_d // 2
        us = down_projection_weight.shape[0] // DP
        gain_one, gain_two = attention_gain[None], feedforward_gain[None]
        a = d // J

        xs = [reshard(tokens[i * n // 2 : (i + 1) * n // 2, 0]) for i in (0, 1)]

        wq_own = qkv_weight.transpose(1, 0, 2)
        f = wq_own.shape[2]
        share = jnp.concatenate(
            [
                lax.dynamic_slice_in_dim(wq_own, pair * a, a, 1),
                lax.dynamic_slice_in_dim(output_projection_weight, pair * a, a, 1)[None],
            ],
            axis=0,
        )
        far_pairs = [
            ((2 * j + 1) * T + t, (2 * j + 1) * T + (t + R) % T)
            for j in range(J)
            for t in range(T)
        ]
        share = lax.ppermute(after(share, xs[0]), ("dp", "tensor"), far_pairs)
        shares = [share] + [
            lax.ppermute(
                share, "dp", [(2 * j + 1, 2 * (j ^ k) + 1) for j in range(J)]
            )
            for k in range(1, J)
        ]
        index = jnp.stack([pair ^ k for k in range(J)] + [core]).astype(jnp.int32)
        pack = pack_call(index, wq_own, output_projection_weight, shares)

        positions = jnp.arange(length, dtype=jnp.int32)
        valid = (positions < window_lengths[0]) & (key_mask[:, 0] == 1)
        bias_own = jnp.where(valid, 0.0, MASKED).astype(F32)
        bias = jnp.where(core == h, bias_own, core_flip(bias_own))
        order = jnp.stack(
            [((core + dc) % 2) * R + (r + dr) % R for dr in range(R) for dc in (0, 1)]
        )
        bias = jnp.take(bias.reshape(T, n), order, axis=0).reshape(length)
        bias = jnp.concatenate(
            [bias[None].astype(BF16), jnp.zeros((15, length), BF16)], axis=0
        )
        places = (order[:, None] * n + jnp.arange(n, dtype=jnp.int32)[None]).reshape(length)
        half = HEAD_DIM // 2
        frequencies = ROPE_BASE ** (-(jnp.arange(half, dtype=F32) * 2.0 / HEAD_DIM))
        angles = frequencies[:, None] * places.astype(F32)[None]
        cos, sin = jnp.cos(angles), jnp.sin(angles)

        gate, up = lax.dynamic_slice_in_dim(gate_up_weight, me_d * us, us, 2).transpose(1, 2, 0)
        dn = lax.dynamic_slice_in_dim(down_projection_weight, me_d * us, us, 0)

        xs[0], _ = lax.optimization_barrier((xs[0], (bias, cos, sin, gate, up, index)))
        first = norm_call(xs[0], gain_one)
        rows_one = send_rows(first)
        second = norm_call(after(xs[1], first), gain_one)
        rows_two = send_rows(second)
        flips = [core_flip(first), core_flip(second)]
        normed_one = gather_heads(first, flips[0], rows_one, second)
        normed_one += gather_heads(second, flips[1], rows_two, pack)
        x = jnp.concatenate(xs)
        cot = reshard(after(cotangent[:, 0], xs[1]))

        gate, up, dn = [
            lax.all_gather(z, "tensor", axis=0) for z in tie(gate, up, dn, second)[:3]
        ]
        own_units = (gate, up, dn)
        weights = [own_units] + [[mid_from(z, k) for z in own_units] for k in range(1, M)]
        q, k, v = qkv_call(normed_one, pack, cos, sin)
        heads = f // HEAD_DIM
        count = max(1, heads // 2)
        o, lse = [], []
        for first in range(0, heads, count):
            if first:
                q, o[0] = tie(q, o[0])
            got = attend_call(q, k, v, bias, first, count)
            o.append(got[0])
            lse.append(got[1])
        o[-1], cot = tie(o[-1], cot)
        pieces = out_call(o, pack, T, d)
        cots = gather_units(after(cot, pieces[0]))
        arrived = scatter_heads(pieces)
        middle, normed = middle_call(x, gain_two, arrived)

        xs = gather_units(normed)
        near = ffn_call(xs[:2], cots[:2], weights)
        near_dx = core_flip(near[6])
        far_x, near_dx = tie(xs[2], near_dx)
        far = ffn_call([far_x, xs[3]], cots[2:], weights)

        def cross(mine, theirs):
            both = mine.astype(F32) + core_flip(theirs).astype(F32)
            return top_flip(both.astype(BF16))

        crossed = cross(far[5], far[6])

        def weight_grads(m, hold):
            return ffn_weight_call(
                [after(xs[0], hold), *xs[1:]], cots, *[[near[i], far[i]] for i in range(3)], m, T, us
            )

        sent, hold = [], far[0]
        for m in range(M - 1, 0, -1):
            got = weight_grads(m, hold)
            hold = got[0]
            sent.append([mid_from(g, M - m) for g in got])
        crossed, _ = tie(crossed, hold)
        middle_grad, middle_low, gain_two_part = back_call(
            "middle_grad", cot, middle, gain_two, [near[5], near_dx, crossed], 1
        )
        low_rows = send_rows(middle_low)
        flipped = core_flip(middle_low)
        own_grads = weight_grads(0, flipped)
        out_crossed = cross(after(far[3], flipped), far[4])

        def total(i, hold):
            t = after(own_grads[i], hold).astype(F32)
            for z in sent:
                t = t + z[i].astype(F32)
            return t.astype(BF16)

        def reduce_rows(g):
            return lax.psum_scatter(g, "tensor", scatter_dimension=0)

        first_sum = total(0, own_grads[0])
        first_part = reduce_rows(first_sum)
        lows = gather_heads(middle_low, flipped, low_rows, first_sum)
        g, wo_grad = heads_grad_call(o, pack, lows)

        back = []
        for i in range(heads):
            if i == 1:
                near_out = core_flip(after(near[4], g))
                output = output_call(after(middle, back[0][0]), [near[3], near_out, out_crossed])
                moved_output = reshard(output)
                second_sum = total(1, output)
                g, second_sum = tie(g, second_sum)
                second_part = reduce_rows(second_sum)
            elif i:
                g = after(g, back[-1][0])
            if i == heads - 1:
                g, first_part = tie(g, first_part)
            j = i // count
            back.append(
                attend_back_call(q, k, v, bias, o[j], lse[j], g, cos, sin, i, i - j * count)
            )
        wo_grad, _ = tie(wo_grad, back[-1][0])
        dw = qkv_weight_call(wo_grad, back, normed_one, pack.shape)
        pieces = qkv_back_call(after(pack, dw), back, T, d)
        second_part, *pieces = tie(second_part, *pieces)
        slices = jnp.concatenate([first_part[None], second_part])
        slices = lax.all_gather(slices, "dp", axis=0)

        def share_of(k):
            return lax.dynamic_index_in_dim(dw, pair ^ k, 0, keepdims=False)

        travelled = [pair_from(share_of(k), k) for k in range(1, J)]
        arrived = scatter_heads(pieces)
        part = share_of(0).astype(F32)
        for p in travelled:
            part = part + p.astype(F32)
        part = part.astype(BF16)
        home_pairs = [
            ((2 * j + 1) * T + t, 2 * j * T + (t + R) % T) for j in range(J) for t in range(T)
        ]
        moved = lax.ppermute(part, ("dp", "tensor"), home_pairs)
        part = (part.astype(F32) + moved.astype(F32)).astype(BF16)
        part = jnp.where(core == 0, part, core_flip(part))
        shares = [part] + [pair_from(part, k) for k in range(1, J)]

        tokens_low, gain_one_part = back_call(
            "tokens_grad", middle_grad, x, gain_one, arrived, 0
        )
        tokens_grad = reshard(tokens_low)[:, None]
        gains = jnp.concatenate([gain_one_part, gain_two_part], axis=0)
        gains = sum_all(after(gains, part))
        gate_up_grad, down_grad = assemble_call(after(slices, gains))
        qkv_grad, out_grad = unpack_call(after(index, down_grad), shares)
        qkv_grad = qkv_grad.transpose(1, 0, 2)
        return (
            moved_output[:, None], tokens_grad, qkv_grad, out_grad, gate_up_grad, down_grad, gains[0], gains[1]
        )

    return on_device


def solution(mesh):
    return jax.shard_map(
        build(mesh.shape["dp"], mesh.shape["tensor"]),
        mesh=mesh,
        in_specs=(
            P("tensor", "dp", None),
            P(None, None, "tensor"),
            P("tensor", None),
            P(None, None, "tensor"),
            P("tensor", None),
            P(),
            P(),
            P("dp"),
            P(None, "dp"),
            P("tensor", "dp", None),
        ),
        out_specs=(
            P("tensor", "dp", None),
            P("tensor", "dp", None),
            P(None, None, "tensor"),
            P("tensor", None),
            P(None, None, "tensor"),
            P("tensor", None),
            P(),
            P(),
        ),
        check_vma=False,
    )
```

```python
import functools
import math

import jax
import jax.numpy as jnp
from jax import lax
from jax.experimental import pallas as pl
from jax.experimental.pallas import tpu as pltpu
from jax.sharding import PartitionSpec as P

HEAD_DIM = 64
EPSILON = 1e-05
MASKED = -1000000000.0
ROPE_BASE = 10000.0
LOG2E = math.log2(math.e)
SCALE = HEAD_DIM ** (-0.5)
BF16 = jnp.bfloat16
F32 = jnp.float32
MIB = 1 << 20
PER_US = 1.15e9 * 0.25


def dot(a, b, ca, cb):
    return lax.dot_general(a, b, (((ca,), (cb,)), ((), ())), preferred_element_type=F32)


def call(body, name, out, us, vmem=56, **kw):
    return pl.pallas_call(
        body,
        out_shape=out,
        name=name,
        compiler_params=pltpu.CompilerParams(vmem_limit_bytes=vmem * MIB),
        cost_estimate=pl.CostEstimate(
            flops=int(us * PER_US), bytes_accessed=0, transcendentals=0
        ),
        **kw,
    )


def shape(s, d):
    return jax.ShapeDtypeStruct(s, d)


def norm_rows(x, gain):
    centered = x - jnp.mean(x, axis=-1, keepdims=True)
    inverse = lax.rsqrt(jnp.mean(centered * centered, axis=-1, keepdims=True) + EPSILON)
    scaled = centered * inverse
    return scaled * gain, scaled, inverse


def norm_kernel(x_ref, g_ref, o_ref):
    o_ref[...] = norm_rows(x_ref[...].astype(F32), g_ref[...])[0].astype(BF16)


def norm_call(x, gain):
    n, d = x.shape
    b = min(128, n)
    return call(
        norm_kernel,
        "norm_tokens",
        shape((n, d), BF16),
        grid=(n // b,),
        in_specs=[pl.BlockSpec((b, d), lambda i: (i, 0)), pl.BlockSpec((1, d), lambda i: (0, 0))],
        out_specs=pl.BlockSpec((b, d), lambda i: (i, 0)),
        us=2.2,
    )(x, gain)


def middle_kernel(x_ref, g_ref, *refs):
    parts, (m_ref, o_ref) = refs[:-2], refs[-2:]
    m = x_ref[...].astype(F32)
    for p in parts:
        m = m + p[...].astype(F32)
    m_ref[...] = m
    o_ref[...] = norm_rows(m, g_ref[...])[0].astype(BF16)


def middle_call(x, gain, parts):
    n, d = x.shape
    b = min(128, n)
    row = pl.BlockSpec((b, d), lambda i: (i, 0))
    return call(
        middle_kernel,
        "middle_norm",
        (shape((n, d), F32), shape((n, d), BF16)),
        grid=(n // b,),
        in_specs=[row, pl.BlockSpec((1, d), lambda i: (0, 0))] + [row] * len(parts),
        out_specs=(row, row),
        us=4.5,
    )(x, gain, *parts)


def back_kernel(n_parts, keep, base_ref, x_ref, g_ref, *refs):
    parts, outs = refs[:n_parts], refs[n_parts:]
    e = parts[0][...].astype(F32)
    for p in parts[1:]:
        e = e + p[...].astype(F32)
    gain = g_ref[...]
    _, scaled, inverse = norm_rows(x_ref[...].astype(F32), gain)
    through = e * gain
    first = jnp.mean(through, axis=-1, keepdims=True)
    second = jnp.mean(through * scaled, axis=-1, keepdims=True)
    total = base_ref[...].astype(F32) + inverse * (through - first - scaled * second)
    if keep:
        outs[0][...] = total
    outs[-1][...] = total.astype(BF16)


def back_call(name, base, x, gain, parts, keep):
    n, d = x.shape
    b = min(256, n)
    row = pl.BlockSpec((b, d), lambda i: (i, 0))
    one = pl.BlockSpec((1, d), lambda i: (0, 0))
    return call(
        functools.partial(back_kernel, len(parts), keep),
        name,
        [shape((n, d), F32)] * keep + [shape((n, d), BF16)],
        us=5,
        grid=(n // b,),
        in_specs=[row, row, one] + [row] * len(parts),
        out_specs=[row] * (keep + 1),
    )(base, x, gain, *parts)


def output_kernel(m_ref, *refs):
    total = m_ref[...]
    for p in refs[:-1]:
        total = total + p[...].astype(F32)
    refs[-1][...] = total.astype(BF16)


def output_call(m, parts):
    n, d = m.shape
    b = min(256, n)
    row = pl.BlockSpec((b, d), lambda i: (i, 0))
    return call(
        output_kernel,
        "output_sum",
        shape((n, d), BF16),
        grid=(n // b,),
        in_specs=[row] * (1 + len(parts)),
        out_specs=row,
        us=3.6,
    )(m, *parts)


def turn(u, cos, sin):
    half = HEAD_DIM // 2
    first, second = u[:half], u[half:]
    return jnp.concatenate([first * cos - second * sin, second * cos + first * sin], axis=0)


def turn_back(u, cos, sin):
    half = HEAD_DIM // 2
    first, second = u[:half], u[half:]
    return jnp.concatenate([first * cos + second * sin, second * cos - first * sin], axis=0)


def part_cols(i, n_parts, n):
    at = (i % (n_parts // 2)) * 2 + i // (n_parts // 2)
    return slice(at * n, (at + 1) * n)


def qkv_kernel(n_parts, c_ref, s_ref, w_ref, *refs):
    parts, (q_ref, k_ref, v_ref) = refs[:n_parts], refs[n_parts:]
    n, d = parts[0].shape
    f = w_ref.shape[-1]
    for which, out in enumerate((q_ref, k_ref, v_ref)):
        w = w_ref[:, which].reshape(d, f)
        for i, p in enumerate(parts):
            cols = part_cols(i, n_parts, n)
            cos, sin = c_ref[:, cols], s_ref[:, cols]
            u = dot(w, p[...], 0, 1)
            for h in range(f // HEAD_DIM):
                rows = slice(h * HEAD_DIM, (h + 1) * HEAD_DIM)
                head = u[rows]
                if which < 2:
                    head = turn(head, cos, sin)
                out[rows, cols] = head.astype(BF16)


def qkv_call(parts, pack, cos, sin):
    n, d = parts[0].shape
    f = pack.shape[-1]
    total = n * len(parts)
    return call(
        functools.partial(qkv_kernel, len(parts)),
        "project_heads",
        (shape((f, total), BF16),) * 3,
        us=7.6,
    )(cos, sin, pack, *parts)


def split(x, n):
    out = []
    for _ in range(n):
        h = x.astype(BF16)
        out.append(h)
        x = x - h.astype(F32)
    return out


def attend_kernel(q_ref, k_ref, v_ref, b_ref, o_ref, l_ref, ka, va, *, sub):
    S = k_ref.shape[1]
    bq = q_ref.shape[1]

    @pl.when(pl.program_id(1) == 0)
    def _():
        k = k_ref[...]
        ka[...] = jnp.concatenate([k, k, b_ref[...]], axis=0).T
        va[0:HEAD_DIM] = v_ref[...]
        va[HEAD_DIM:] = jnp.ones((16, S), BF16)

    high, low = split(q_ref[...].astype(F32) * (SCALE * LOG2E), 2)
    row = lax.broadcasted_iota(jnp.int32, (16, bq), 0)
    one = jnp.where(row == 0, 1.0, 0.0).astype(BF16)
    qa = jnp.concatenate([high, low, one], axis=0)
    steps = bq // sub

    def scores(i):
        return dot(ka[...], qa[:, i * sub : (i + 1) * sub], 1, 0)

    s = scores(0)
    for i in range(steps):
        later = scores(i + 1) if i + 1 < steps else None
        cols = slice(i * sub, (i + 1) * sub)
        top = jnp.max(s, axis=0, keepdims=True)
        p = jnp.exp2(s - top).astype(BF16)
        o = dot(va[...], p, 1, 0)
        total = o[HEAD_DIM : HEAD_DIM + 1]
        o_ref[:, cols] = (o[:HEAD_DIM] * (1.0 / total)).astype(BF16)
        l_ref[0, :, cols] = jnp.broadcast_to(top + jnp.log2(total), (8, sub))
        s = later


def attend_call(q, k, v, bias, first, count):
    S = q.shape[1]
    bq = S
    sub = min(256, S)
    whole = pl.BlockSpec((HEAD_DIM, S), lambda h, i: (h + first, 0))
    block = pl.BlockSpec((HEAD_DIM, bq), lambda h, i: (h + first, i))
    return call(
        functools.partial(attend_kernel, sub=sub),
        "attend",
        (shape((count * HEAD_DIM, S), BF16), shape((count, 8, S), F32)),
        grid=(count, S // bq),
        in_specs=[block, whole, whole, pl.BlockSpec((16, S), lambda h, i: (0, 0))],
        out_specs=(
            pl.BlockSpec((HEAD_DIM, bq), lambda h, i: (h, i)),
            pl.BlockSpec((1, 8, bq), lambda h, i: (h, 0, i)),
        ),
        scratch_shapes=[
            pltpu.VMEM((S, 2 * HEAD_DIM + 16), BF16),
            pltpu.VMEM((HEAD_DIM + 16, S), BF16),
        ],
        us=7.4 * count,
    )(q, k, v, bias)


def attend_back_kernel(
    q_ref, k_ref, v_ref, b_ref, o_ref, l_ref, g_ref, c_ref, s_ref, ck_ref, sk_ref,
    dq_ref, dk_ref, dv_ref, ka, va, dka, dva, *, sub
):
    S = k_ref.shape[1]
    bq = q_ref.shape[1]

    @pl.when(pl.program_id(1) == 0)
    def _():
        k = k_ref[...]
        one = jnp.ones((16, S), BF16)
        ka[...] = jnp.concatenate([k, k, b_ref[...], one], axis=0).T
        va[...] = jnp.concatenate([v_ref[...], one], axis=0).T
        dka[...] = jnp.zeros_like(dka)
        dva[...] = jnp.zeros_like(dva)

    q = q_ref[...].astype(F32) * SCALE
    qs = q.astype(BF16)
    high, low = split(q * LOG2E, 2)
    row = lax.broadcasted_iota(jnp.int32, (16, bq), 0)

    def spread(x):
        a, b, c = [y.astype(F32) for y in split(x, 3)]
        rest = jnp.where(row == 2, c, 0.0)
        return jnp.where(row == 0, a, jnp.where(row == 1, b, rest)).astype(BF16)

    one = jnp.where(row == 0, 1.0, 0.0).astype(BF16)
    g = g_ref[...]
    qa = jnp.concatenate([high, low, one, spread(-l_ref[0, 0:1])], axis=0)
    centre = jnp.sum(g.astype(F32) * o_ref[...].astype(F32), axis=0, keepdims=True)
    ga = jnp.concatenate([g, spread(-centre)], axis=0)
    for i in range(bq // sub):
        cols = slice(i * sub, (i + 1) * sub)
        p = jnp.exp2(dot(ka[...], qa[:, cols], 1, 0))
        p_low = p.astype(BF16)
        ds = (p * dot(va[...], ga[:, cols], 1, 0)).astype(BF16)
        dva[...] += dot(g[:, cols], p_low, 1, 1)
        dka[...] += dot(qs[:, cols], ds, 1, 1)
        dq = dot(k_ref[...], ds, 1, 0) * SCALE
        dq_ref[:, cols] = turn_back(dq, c_ref[:, cols], s_ref[:, cols]).astype(BF16)

    @pl.when(pl.program_id(1) == pl.num_programs(1) - 1)
    def _():
        dk_ref[...] = turn_back(dka[...], ck_ref[...], sk_ref[...]).astype(BF16)
        dv_ref[...] = dva[...].astype(BF16)


def attend_back_call(q, k, v, bias, o, lse, g, cos, sin, head, place):
    S = q.shape[1]
    bq = min(1024, S)
    half = HEAD_DIM // 2
    whole = pl.BlockSpec((HEAD_DIM, S), lambda h, i: (head, 0))
    block = pl.BlockSpec((HEAD_DIM, bq), lambda h, i: (head, i))
    table = pl.BlockSpec((half, S), lambda h, i: (0, 0))
    table_block = pl.BlockSpec((half, bq), lambda h, i: (0, i))
    return call(
        functools.partial(attend_back_kernel, sub=min(256, S)),
        "attend_back",
        (shape((HEAD_DIM, S), BF16),) * 3,
        us=12.3,
        grid=(1, S // bq),
        in_specs=[
            block, whole, whole,
            pl.BlockSpec((16, S), lambda h, i: (0, 0)),
            pl.BlockSpec((HEAD_DIM, bq), lambda h, i: (place, i)),
            pl.BlockSpec((1, 8, bq), lambda h, i: (place, 0, i)),
            block, table_block, table_block, table, table,
        ],
        out_specs=(
            pl.BlockSpec((HEAD_DIM, bq), lambda h, i: (0, i)),
            pl.BlockSpec((HEAD_DIM, S), lambda h, i: (0, 0)),
            pl.BlockSpec((HEAD_DIM, S), lambda h, i: (0, 0)),
        ),
        scratch_shapes=[
            pltpu.VMEM((S, 2 * HEAD_DIM + 32), BF16),
            pltpu.VMEM((S, HEAD_DIM + 16), BF16),
            pltpu.VMEM((HEAD_DIM, S), F32),
            pltpu.VMEM((HEAD_DIM, S), F32),
        ],
    )(q, k, v, bias, o, lse, g, cos, sin, cos, sin)


def stack_rows(refs, cols):
    return jnp.concatenate([r[:, cols] for r in refs], axis=0)


def out_kernel(n_heads, w_ref, *refs):
    heads, outs = refs[:n_heads], refs[n_heads:]
    n, d = outs[0].shape
    J, b = w_ref.shape[0], w_ref.shape[-1]
    for i, out in enumerate(outs):
        o = stack_rows(heads, slice(i * n, (i + 1) * n))
        for j in range(J):
            out[:, j * b : (j + 1) * b] = dot(o, w_ref[j], 0, 0).astype(BF16)


def pack_spec(pack, which):
    J, _, a, b = pack.shape
    return pl.BlockSpec((J, None, a, b), lambda i: (0, which, 0, 0))


def full(s):
    return pl.BlockSpec(s, lambda i: (0,) * len(s))


def out_call(heads, pack, n_parts, d):
    S = heads[0].shape[1]
    f = sum(o.shape[0] for o in heads)
    return call(
        functools.partial(out_kernel, len(heads)),
        "output_projection",
        (shape((S // n_parts, d), BF16),) * n_parts,
        grid=(1,),
        in_specs=[pack_spec(pack, 3)] + [full(o.shape) for o in heads],
        out_specs=(full((S // n_parts, d)),) * n_parts,
        us=4.2,
    )(pack, *heads)


def heads_grad_kernel(n_heads, n_parts, w_ref, *refs):
    heads, parts, (g_ref, dw_ref) = (
        refs[:n_heads], refs[n_heads : n_heads + n_parts], refs[n_heads + n_parts :]
    )
    n = parts[0].shape[0]
    J, b = w_ref.shape[0], w_ref.shape[-1]
    w = jnp.concatenate([w_ref[j] for j in range(J)], axis=1)
    total = None
    for i, p in enumerate(parts):
        cols = slice(i * n, (i + 1) * n)
        g_ref[:, cols] = dot(w, p[...], 1, 1).astype(BF16)
        term = dot(stack_rows(heads, cols), p[...], 1, 0)
        total = term if total is None else total + term
    for j in range(J):
        dw_ref[j] = total[:, j * b : (j + 1) * b].astype(BF16)


def heads_grad_call(heads, pack, parts):
    S = heads[0].shape[1]
    f = sum(o.shape[0] for o in heads)
    n, d = parts[0].shape
    J, _, a, b = pack.shape
    return call(
        functools.partial(heads_grad_kernel, len(heads), len(parts)),
        "heads_grad",
        (shape((f, S), BF16), shape((J, a, b), BF16)),
        grid=(1,),
        in_specs=[pack_spec(pack, 3)] + [full(o.shape) for o in heads] + [full((n, d))] * len(parts),
        out_specs=(full((f, S)), full((J, a, b))),
        us=6,
    )(pack, *heads, *parts)


def qkv_back_kernel(n_parts, n_groups, w_ref, *refs):
    grads, outs = refs[: 3 * n_groups], refs[3 * n_groups :]
    n, d = outs[0].shape
    f = w_ref.shape[-1]
    for i, out in enumerate(outs):
        cols = slice(i * n, (i + 1) * n)
        total = None
        for j in range(3):
            g = stack_rows(grads[j::3], cols)
            term = dot(g, w_ref[:, j].reshape(d, f), 0, 1)
            total = term if total is None else total + term
        out[...] = total.astype(BF16)


def qkv_back_call(pack, grads, n_parts, d):
    f = pack.shape[-1]
    S = grads[0][0].shape[1]
    flat = [g for group in grads for g in group]
    return call(
        functools.partial(qkv_back_kernel, n_parts, len(grads)),
        "qkv_back",
        (shape((S // n_parts, d), BF16),) * n_parts,
        us=7,
    )(pack, *flat)


def qkv_weight_kernel(n_parts, n_groups, wo_ref, *refs):
    grads, parts, dw_ref = refs[: 3 * n_groups], refs[3 * n_groups : -1], refs[-1]
    n = parts[0].shape[0]
    J, _, a, b = dw_ref.shape
    for j in range(3):
        total = None
        for i, p in enumerate(parts):
            g = stack_rows(grads[j::3], part_cols(i, n_parts, n))
            term = dot(p[...], g, 0, 1)
            total = term if total is None else total + term
        dw_ref[:, j] = total.astype(BF16).reshape(J, a, b)
    dw_ref[:, 3] = wo_ref[...]


def qkv_weight_call(wo_grad, grads, parts, pack_shape):
    n, d = parts[0].shape
    f = pack_shape[-1]
    S = n * len(parts)
    flat = [g for group in grads for g in group]
    return call(
        functools.partial(qkv_weight_kernel, len(parts), len(grads)),
        "qkv_weights",
        shape(pack_shape, BF16),
        us=8,
    )(wo_grad, *flat, *parts)


def pack_kernel(n_parts, index_ref, q_ref, o_ref, *refs):
    parts, out = refs[:-1], refs[-1]
    J, _, a, b = out.shape

    @pl.when(index_ref[n_parts] == 0)
    def _():
        for j in range(J):
            for which in range(3):
                out[j, which] = q_ref[which, j * a : (j + 1) * a]
            out[j, 3] = o_ref[:, j * b : (j + 1) * b]

    @pl.when(index_ref[n_parts] == 1)
    def _():
        for i, p in enumerate(parts):
            out[index_ref[i]] = p[...]


def pack_call(index, wq, wo, parts):
    _, a, b = parts[0].shape
    J = len(parts)
    vmem = pl.BlockSpec(memory_space=pltpu.VMEM)
    return call(
        functools.partial(pack_kernel, J),
        "pack_heads",
        shape((J, 4, a, b), BF16),
        in_specs=[pl.BlockSpec(memory_space=pltpu.SMEM)] + [vmem] * (J + 2),
        out_specs=vmem,
        us=3.7,
    )(index, wq, wo, *parts)


def column_sums(x):
    return jnp.sum(x.T, axis=0, keepdims=True)


def unpack_kernel(n_parts, index_ref, w_ref, *refs):
    parts, (q_ref, o_ref, gain_ref) = refs[:n_parts], refs[n_parts:]
    a, b = parts[0].shape[1:]
    for i, p in enumerate(parts):
        j = index_ref[i]
        rows = pl.ds(pl.multiple_of(j * a, a), a)
        gain = None
        for which in range(3):
            g = p[which].astype(F32)
            q_ref[which, rows, :] = g
            term = g * w_ref[which, rows, :].astype(F32)
            gain = term if gain is None else gain + term
        o_ref[:, pl.ds(pl.multiple_of(j * b, b), b)] = p[3].astype(F32)
        gain_ref[:, rows] = column_sums(gain)


def unpack_call(index, wq, parts):
    _, a, b = parts[0].shape
    J = len(parts)
    vmem = pl.BlockSpec(memory_space=pltpu.VMEM)
    return call(
        functools.partial(unpack_kernel, J),
        "unpack_heads",
        (shape((3, J * a, b), F32), shape((a, J * b), F32), shape((1, J * a), F32)),
        in_specs=[pl.BlockSpec(memory_space=pltpu.SMEM)] + [vmem] * (J + 1),
        out_specs=(vmem, vmem, vmem),
        us=3.8,
    )(index, wq, *parts)


def ffn_kernel(groups, steps, *refs):
    x0, x1, c0, c1 = refs[:4]
    weights = refs[4 : 4 + 3 * groups]
    h_ref, gl_ref, ul_ref, out0, out1, dx0, dx1 = refs[4 + 3 * groups :]
    early = pl.program_id(0) < steps
    x = jnp.where(early, x0[...], x1[...])
    c = jnp.where(early, c0[...], c1[...])
    out = dx = None
    for m in range(groups):
        wg, wu, wd = [r[...].reshape(-1, r.shape[-1]) for r in weights[3 * m : 3 * m + 3]]
        gate = dot(x, wg, 1, 1)
        up = dot(x, wu, 1, 1)
        hg = dot(c, wd, 1, 1)
        sig = jax.nn.sigmoid(gate)
        act = gate * sig
        hidden = (act * up).astype(BF16)
        gl = (hg * up * (sig * (1.0 + gate * (1.0 - sig)))).astype(BF16)
        ul = (hg * act).astype(BF16)
        cols = slice(m * wg.shape[0], (m + 1) * wg.shape[0])
        h_ref[:, cols] = hidden
        gl_ref[:, cols] = gl
        ul_ref[:, cols] = ul
        o = dot(hidden, wd, 1, 0)
        e = dot(gl, wg, 1, 0) + dot(ul, wu, 1, 0)
        out = o if out is None else out + o
        dx = e if dx is None else dx + e

    @pl.when(early)
    def _():
        out0[...] = out.astype(BF16)
        dx0[...] = dx.astype(BF16)

    @pl.when(jnp.logical_not(early))
    def _():
        out1[...] = out.astype(BF16)
        dx1[...] = dx.astype(BF16)


def ffn_call(xs, cs, weights):
    n, d = xs[0].shape
    groups = len(weights)
    T, us, _ = weights[0][0].shape
    units = groups * T * us
    b = min(256, n)
    steps = n // b
    first = pl.BlockSpec((b, d), lambda i: (jnp.minimum(i, steps - 1), 0))
    second = pl.BlockSpec((b, d), lambda i: (jnp.maximum(i - steps, 0), 0))
    urow = pl.BlockSpec((b, units), lambda i: (i, 0))
    specs, args = [], []
    for group in weights:
        specs += [pl.BlockSpec((T, us, d), lambda i: (0, 0, 0))] * 3
        args += group
    return call(
        functools.partial(ffn_kernel, groups, steps),
        "feed_forward",
        (shape((2 * n, units), BF16),) * 3 + (shape((n, d), BF16),) * 4,
        grid=(2 * steps,),
        in_specs=[first, second, first, second] + specs,
        out_specs=(urow,) * 3 + (first, second, first, second),
        us=21,
    )(*xs, *cs, *args)


def ffn_weight_kernel(T, us, *refs):
    x, c = refs[:4], refs[4:8]
    h, gl, ul = refs[8:10], refs[10:12], refs[12:14]
    outs = refs[14:]
    n = x[0].shape[0]

    def product(a, b):
        total = None
        for i in range(4):
            rows = slice((i % 2) * n, (i % 2 + 1) * n)
            term = dot(a[i][...], b(i, rows), 0, 0)
            total = term if total is None else total + term
        return total.astype(BF16)

    dw = product(c, lambda i, rows: h[i // 2][rows])
    for t in range(T):
        outs[0][t, 2] = dw[:, t * us : (t + 1) * us]
    dw = product(x, lambda i, rows: jnp.concatenate([gl[i // 2][rows], ul[i // 2][rows]], axis=1))
    for j in range(2):
        for t in range(T):
            at = (j * T + t) * us
            outs[0][t, j] = dw[:, at : at + us]


def ffn_weight_call(x, c, h, gl, ul, m, T, us):
    n, d = x[0].shape
    db = min(256, d)
    spec = [pl.BlockSpec((n, db), lambda i: (0, i))] * 8
    spec += [pl.BlockSpec((2 * n, T * us), lambda i: (0, m))] * 6
    return call(
        functools.partial(ffn_weight_kernel, T, us),
        "feed_forward_weights",
        shape((T, 3, d, us), BF16),
        grid=(d // db,),
        in_specs=spec,
        out_specs=pl.BlockSpec((T, 3, db, us), lambda i: (0, 0, i, 0)),
        us=12.4,
    )(*x, *c, *h, *gl, *ul)


def assemble_kernel(w_ref, old_ref, gu_ref, dn_ref, gain_ref):
    DP, _, _, us = w_ref.shape
    gain = None
    for j in range(2):
        rows = jnp.concatenate([w_ref[p, j] for p in range(DP)], axis=1).astype(F32)
        gu_ref[:, j, :] = rows
        term = rows * old_ref[:, j, :].astype(F32)
        gain = term if gain is None else gain + term
    gain_ref[...] = column_sums(gain)
    rows = jnp.concatenate([w_ref[p, 2] for p in range(DP)], axis=1)
    dn_ref[...] = rows.T.astype(F32)


def assemble_call(w, old):
    DP, _, d, us = w.shape
    b = min(256, d)
    return call(
        assemble_kernel,
        "feed_forward_gradients",
        (shape((d, 2, DP * us), F32), shape((DP * us, d), F32), shape((1, d), F32)),
        us=9,
        grid=(d // b,),
        in_specs=[
            pl.BlockSpec((DP, 3, b, us), lambda i: (0, 0, i, 0)),
            pl.BlockSpec((b, 2, DP * us), lambda i: (i, 0, 0)),
        ],
        out_specs=(
            pl.BlockSpec((b, 2, DP * us), lambda i: (i, 0, 0)),
            pl.BlockSpec((DP * us, b), lambda i: (0, i)),
            pl.BlockSpec((1, b), lambda i: (0, i)),
        ),
    )(w, old)


def after(x, *deps):
    return lax.optimization_barrier((x, *deps))[0]


def tie(*xs):
    return lax.optimization_barrier(xs)


def build(DP, T):
    M = DP // 4
    R = T // 2
    J = DP // 2

    def over_dp(x, f):
        return lax.ppermute(x, "dp", [(i, f(i)) for i in range(DP)])

    def core_flip(x):
        return over_dp(x, lambda i: i ^ 1)

    def top_flip(x):
        return over_dp(x, lambda i: (i + DP // 2) % DP)

    def mid_from(x, k):
        def dest(i):
            a, m, c = i // (DP // 2), (i // 2) % M, i % 2
            return a * (DP // 2) + ((m - k) % M) * 2 + c

        return over_dp(x, dest)

    def pair_from(x, k):
        return over_dp(x, lambda i: ((i // 2) ^ k) * 2 + i % 2)

    def row_from(x, k):
        return lax.ppermute(
            x, "tensor", [((t // R) * R + (t % R + k) % R, t) for t in range(T)]
        )

    def reshard(x):
        pairs = []
        for d in range(DP):
            for t in range(T):
                j, c, h, r = d // 2, d % 2, t // R, t % R
                pairs.append((d * T + t, (2 * j + h) * T + c * R + r))
        return lax.ppermute(x, ("dp", "tensor"), pairs)

    def send_rows(x):
        return [row_from(x, k) for k in range(1, R)]

    def gather_heads(x, flipped, rows, hold):
        out = [x, flipped]
        for y in rows:
            y = after(y, hold)
            out += [y, core_flip(y)]
        return out

    def sum_heads(pieces):
        flips = [core_flip(z) for z in pieces[1::2]]
        sums = [
            (pieces[2 * k].astype(F32) + flips[k].astype(F32)).astype(BF16) for k in range(1, R)
        ]
        return sums, [pieces[0], flips[0]]

    def scatter_heads(pieces):
        out = []
        for k in range(R):
            mine, theirs = pieces[2 * k], core_flip(pieces[2 * k + 1])
            if k == 0:
                out += [mine, theirs]
            else:
                both = (mine.astype(F32) + theirs.astype(F32)).astype(BF16)
                out.append(row_from(both, R - k))
        return out

    def gather_units(y):
        z = top_flip(y)
        return [y, core_flip(y), z, core_flip(z)]

    def sum_rows(x):
        for bit in range(T.bit_length() - 1):
            x = x + lax.ppermute(x, "tensor", [(t, t ^ (1 << bit)) for t in range(T)])
        return x

    def on_device(
        tokens, qkv_weight, output_projection_weight, gate_up_weight, down_projection_weight,
        attention_gain, feedforward_gain, window_lengths, key_mask, cotangent,
    ):
        n, _, d = tokens.shape
        length = key_mask.shape[0]
        me_d, me_t = lax.axis_index("dp"), lax.axis_index("tensor")
        core, h, r, pair = me_d % 2, me_t // R, me_t % R, me_d // 2
        us = down_projection_weight.shape[0] // DP
        gain_one, gain_two = attention_gain[None], feedforward_gain[None]
        a = d // J

        xs = [reshard(tokens[i * n // 2 : (i + 1) * n // 2, 0]) for i in (0, 1)]

        wq_own = qkv_weight.transpose(1, 0, 2)
        f = wq_own.shape[2]
        share = jnp.concatenate(
            [
                lax.dynamic_slice_in_dim(wq_own, pair * a, a, 1),
                lax.dynamic_slice_in_dim(output_projection_weight, pair * a, a, 1)[None],
            ],
            axis=0,
        )
        far_pairs = [
            ((2 * j + 1) * T + t, (2 * j + 1) * T + (t + R) % T)
            for j in range(J)
            for t in range(T)
        ]
        share = lax.ppermute(after(share, xs[0]), ("dp", "tensor"), far_pairs)
        shares = [share] + [
            lax.ppermute(
                share, "dp", [(2 * j + 1, 2 * (j ^ k) + 1) for j in range(J)]
            )
            for k in range(1, J)
        ]
        index = jnp.stack([pair ^ k for k in range(J)] + [core]).astype(jnp.int32)
        pack = pack_call(index, wq_own, output_projection_weight, shares)

        positions = jnp.arange(length, dtype=jnp.int32)
        valid = (positions < window_lengths[0]) & (key_mask[:, 0] == 1)
        bias_own = jnp.where(valid, 0.0, MASKED).astype(F32)
        bias = jnp.where(core == h, bias_own, core_flip(bias_own))
        order = jnp.stack(
            [((core + dc) % 2) * R + (r + dr) % R for dr in range(R) for dc in (0, 1)]
        )
        bias = jnp.take(bias.reshape(T, n), order, axis=0).reshape(length)
        bias = jnp.concatenate(
            [bias[None].astype(BF16), jnp.zeros((15, length), BF16)], axis=0
        )
        places = (order[:, None] * n + jnp.arange(n, dtype=jnp.int32)[None]).reshape(length)
        half = HEAD_DIM // 2
        frequencies = ROPE_BASE ** (-(jnp.arange(half, dtype=F32) * 2.0 / HEAD_DIM))
        angles = frequencies[:, None] * places.astype(F32)[None]
        cos, sin = jnp.cos(angles), jnp.sin(angles)

        gate, up = lax.dynamic_slice_in_dim(gate_up_weight, me_d * us, us, 2).transpose(1, 2, 0)
        dn = lax.dynamic_slice_in_dim(down_projection_weight, me_d * us, us, 0)

        xs[0], _ = lax.optimization_barrier((xs[0], (bias, cos, sin, gate, up, index)))
        first = norm_call(xs[0], gain_one)
        rows_one = send_rows(first)
        second = norm_call(after(xs[1], first), gain_one)
        rows_two = send_rows(second)
        flips = [core_flip(first), core_flip(second)]
        normed_one = gather_heads(first, flips[0], rows_one, second)
        normed_one += gather_heads(second, flips[1], rows_two, pack)
        x = jnp.concatenate(xs)
        cot = reshard(after(cotangent[:, 0], xs[1]))

        gate, up, dn = [
            lax.all_gather(z, "tensor", axis=0) for z in tie(gate, up, dn, second)[:3]
        ]
        own_units = (gate, up, dn)
        weights = [own_units] + [[mid_from(z, k) for z in own_units] for k in range(1, M)]
        q, k, v = qkv_call(normed_one, pack, cos, sin)
        heads = f // HEAD_DIM
        count = max(1, heads // 2)
        o, lse = [], []
        for first in range(0, heads, count):
            if first:
                q, o[0] = tie(q, o[0])
            got = attend_call(q, k, v, bias, first, count)
            o.append(got[0])
            lse.append(got[1])
        o[-1], cot = tie(o[-1], cot)
        pieces = out_call(o, pack, T, d)
        cots = gather_units(after(cot, pieces[0]))
        arrived = scatter_heads(pieces)
        middle, normed = middle_call(x, gain_two, arrived)

        xs = gather_units(normed)
        near = ffn_call(xs[:2], cots[:2], weights)
        near_dx = core_flip(near[6])
        far_x, near_dx = tie(xs[2], near_dx)
        far = ffn_call([far_x, xs[3]], cots[2:], weights)

        def core_sum(mine, theirs):
            return (mine.astype(F32) + core_flip(theirs).astype(F32)).astype(BF16)

        dx_both = core_sum(far[5], far[6])
        crossed = top_flip(dx_both)

        def weight_grads(m, hold):
            return ffn_weight_call(
                [after(xs[0], hold), *xs[1:]], cots, *[[near[i], far[i]] for i in range(3)], m, T, us
            )

        sent, hold = [], dx_both
        for m in range(M - 1, 0, -1):
            hold = weight_grads(m, hold)
            sent.append(mid_from(hold, M - m))
        out_both = core_sum(after(far[3], hold), far[4])
        near_out = core_flip(after(near[4], hold))
        crossed, out_both, near_out = tie(crossed, out_both, near_out)
        middle_grad, middle_low = back_call(
            "middle_grad", cot, middle, gain_two, [near[5], near_dx, crossed], 1
        )
        low_rows = send_rows(middle_low)
        out_crossed = top_flip(out_both)
        flipped = core_flip(middle_low)
        own_grads = weight_grads(0, flipped)
        output = output_call(after(middle, own_grads), [near[3], near_out, out_crossed])
        lows = gather_heads(middle_low, flipped, low_rows, output)
        moved_output = reshard(output)
        g, wo_grad = heads_grad_call(o, pack, lows)

        back = []
        for i in range(heads):
            if i == 1:
                total = after(own_grads, back[0][0]).astype(F32)
                for z in sent:
                    total = total + z.astype(F32)
                total = total.astype(BF16)
                g, total, moved_output = tie(g, total, moved_output)
                slices = lax.psum_scatter(total, "tensor", scatter_dimension=0)
            elif i:
                g = after(g, back[-1][0])
            j = i // count
            back.append(
                attend_back_call(q, k, v, bias, o[j], lse[j], g, cos, sin, i, i - j * count)
            )
        pieces = qkv_back_call(after(pack, back[-1][0]), back, T, d)
        sums, mine = sum_heads(pieces)
        rows = [row_from(z, R - k) for k, z in enumerate(sums, 1)]
        wo_grad, *sums = tie(wo_grad, *sums)
        dw = qkv_weight_call(wo_grad, back, normed_one, pack.shape)

        def share_of(k):
            return lax.dynamic_index_in_dim(dw, pair ^ k, 0, keepdims=False)

        travelled = [pair_from(share_of(k), k) for k in range(1, J)]
        slices, dw = tie(slices, dw)
        slices = lax.all_gather(slices, "dp", axis=0)
        tokens_low = back_call(
            "tokens_grad", middle_grad, after(x, dw), gain_one, mine + rows, 0
        )[0]
        tokens_grad = reshard(tokens_low)[:, None]
        tokens_low, *travelled = tie(tokens_low, *travelled)
        part = share_of(0).astype(F32)
        for p in travelled:
            part = part + p.astype(F32)
        part = part.astype(BF16)
        home_pairs = [
            ((2 * j + 1) * T + t, 2 * j * T + (t + R) % T) for j in range(J) for t in range(T)
        ]
        moved = lax.ppermute(part, ("dp", "tensor"), home_pairs)
        part = (part.astype(F32) + moved.astype(F32)).astype(BF16)
        part = jnp.where(core == 0, part, core_flip(part))
        shares = [part] + [pair_from(part, k) for k in range(1, J)]

        gate_up_grad, down_grad, gain_two_part = assemble_call(
            after(slices, part), gate_up_weight
        )
        qkv_grad, out_grad, gain_one_part = unpack_call(after(index, down_grad), wq_own, shares)
        qkv_grad = qkv_grad.transpose(1, 0, 2)
        gains = sum_rows(jnp.concatenate([gain_one_part, gain_two_part], axis=0))
        gains = gains / jnp.concatenate([gain_one, gain_two], axis=0)
        return (
            moved_output[:, None], tokens_grad, qkv_grad, out_grad, gate_up_grad, down_grad, gains[0], gains[1]
        )

    return on_device


def solution(mesh):
    return jax.shard_map(
        build(mesh.shape["dp"], mesh.shape["tensor"]),
        mesh=mesh,
        in_specs=(
            P("tensor", "dp", None),
            P(None, None, "tensor"),
            P("tensor", None),
            P(None, None, "tensor"),
            P("tensor", None),
            P(),
            P(),
            P("dp"),
            P(None, "dp"),
            P("tensor", "dp", None),
        ),
        out_specs=(
            P("tensor", "dp", None),
            P("tensor", "dp", None),
            P(None, None, "tensor"),
            P("tensor", None),
            P(None, None, "tensor"),
            P("tensor", None),
            P(),
            P(),
        ),
        check_vma=False,
    )
```

```python
import functools
import math

import jax
import jax.numpy as jnp
from jax import lax
from jax.experimental import pallas as pl
from jax.experimental.pallas import tpu as pltpu
from jax.sharding import PartitionSpec as P

HEAD_DIM = 64
EPSILON = 1e-05
MASKED = -1000000000.0
ROPE_BASE = 10000.0
LOG2E = math.log2(math.e)
SCALE = HEAD_DIM ** (-0.5)
BF16 = jnp.bfloat16
F32 = jnp.float32
MIB = 1 << 20
PER_US = 1.15e9 * 0.25


def dot(a, b, ca, cb):
    return lax.dot_general(a, b, (((ca,), (cb,)), ((), ())), preferred_element_type=F32)


def call(body, name, out, us, vmem=56, **kw):
    return pl.pallas_call(
        body,
        out_shape=out,
        name=name,
        compiler_params=pltpu.CompilerParams(vmem_limit_bytes=vmem * MIB),
        cost_estimate=pl.CostEstimate(
            flops=int(us * PER_US), bytes_accessed=0, transcendentals=0
        ),
        **kw,
    )


def shape(s, d):
    return jax.ShapeDtypeStruct(s, d)


def norm_rows(x, gain):
    centered = x - jnp.mean(x, axis=-1, keepdims=True)
    inverse = lax.rsqrt(jnp.mean(centered * centered, axis=-1, keepdims=True) + EPSILON)
    scaled = centered * inverse
    return scaled * gain, scaled, inverse


def norm_kernel(x_ref, g_ref, o_ref):
    o_ref[...] = norm_rows(x_ref[...].astype(F32), g_ref[...])[0].astype(BF16)


def norm_call(x, gain):
    n, d = x.shape
    b = min(256, n)
    return call(
        norm_kernel,
        "norm_tokens",
        shape((n, d), BF16),
        grid=(n // b,),
        in_specs=[pl.BlockSpec((b, d), lambda i: (i, 0)), pl.BlockSpec((1, d), lambda i: (0, 0))],
        out_specs=pl.BlockSpec((b, d), lambda i: (i, 0)),
        us=2.2,
    )(x, gain)


def middle_kernel(x_ref, g_ref, *refs):
    parts, (m_ref, o_ref) = refs[:-2], refs[-2:]
    m = x_ref[...].astype(F32)
    for p in parts:
        m = m + p[...].astype(F32)
    m_ref[...] = m
    o_ref[...] = norm_rows(m, g_ref[...])[0].astype(BF16)


def middle_call(x, gain, parts):
    n, d = x.shape
    b = min(256, n)
    row = pl.BlockSpec((b, d), lambda i: (i, 0))
    return call(
        middle_kernel,
        "middle_norm",
        (shape((n, d), F32), shape((n, d), BF16)),
        grid=(n // b,),
        in_specs=[row, pl.BlockSpec((1, d), lambda i: (0, 0))] + [row] * len(parts),
        out_specs=(row, row),
        us=4.5,
    )(x, gain, *parts)


def back_kernel(n_parts, keep, base_ref, x_ref, g_ref, *refs):
    parts, outs = refs[:n_parts], refs[n_parts:]
    e = parts[0][...].astype(F32)
    for p in parts[1:]:
        e = e + p[...].astype(F32)
    gain = g_ref[...]
    _, scaled, inverse = norm_rows(x_ref[...].astype(F32), gain)
    through = e * gain
    first = jnp.mean(through, axis=-1, keepdims=True)
    second = jnp.mean(through * scaled, axis=-1, keepdims=True)
    total = base_ref[...].astype(F32) + inverse * (through - first - scaled * second)
    if keep:
        outs[0][...] = total
    outs[-1][...] = total.astype(BF16)


def back_call(name, base, x, gain, parts, keep):
    n, d = x.shape
    b = min(256, n)
    row = pl.BlockSpec((b, d), lambda i: (i, 0))
    one = pl.BlockSpec((1, d), lambda i: (0, 0))
    return call(
        functools.partial(back_kernel, len(parts), keep),
        name,
        [shape((n, d), F32)] * keep + [shape((n, d), BF16)],
        us=5,
        grid=(n // b,),
        in_specs=[row, row, one] + [row] * len(parts),
        out_specs=[row] * (keep + 1),
    )(base, x, gain, *parts)


def output_kernel(m_ref, *refs):
    total = m_ref[...]
    for p in refs[:-1]:
        total = total + p[...].astype(F32)
    refs[-1][...] = total.astype(BF16)


def output_call(m, parts):
    n, d = m.shape
    b = min(256, n)
    row = pl.BlockSpec((b, d), lambda i: (i, 0))
    return call(
        output_kernel,
        "output_sum",
        shape((n, d), BF16),
        grid=(n // b,),
        in_specs=[row] * (1 + len(parts)),
        out_specs=row,
        us=3.6,
    )(m, *parts)


def turn(u, cos, sin):
    half = HEAD_DIM // 2
    first, second = u[:half], u[half:]
    return jnp.concatenate([first * cos - second * sin, second * cos + first * sin], axis=0)


def turn_back(u, cos, sin):
    half = HEAD_DIM // 2
    first, second = u[:half], u[half:]
    return jnp.concatenate([first * cos + second * sin, second * cos - first * sin], axis=0)


def part_cols(i, n_parts, n):
    at = (i % (n_parts // 2)) * 2 + i // (n_parts // 2)
    return slice(at * n, (at + 1) * n)


def qkv_kernel(n_parts, c_ref, s_ref, w_ref, *refs):
    parts, (q_ref, k_ref, v_ref) = refs[:n_parts], refs[n_parts:]
    n, d = parts[0].shape
    f = w_ref.shape[-1]
    for which, out in enumerate((q_ref, k_ref, v_ref)):
        w = w_ref[:, which].reshape(d, f)
        for i, p in enumerate(parts):
            cols = part_cols(i, n_parts, n)
            cos, sin = c_ref[:, cols], s_ref[:, cols]
            u = dot(w, p[...], 0, 1)
            for h in range(f // HEAD_DIM):
                rows = slice(h * HEAD_DIM, (h + 1) * HEAD_DIM)
                head = u[rows]
                if which < 2:
                    head = turn(head, cos, sin)
                out[rows, cols] = head.astype(BF16)


def qkv_call(parts, pack, cos, sin):
    n, d = parts[0].shape
    f = pack.shape[-1]
    total = n * len(parts)
    return call(
        functools.partial(qkv_kernel, len(parts)),
        "project_heads",
        (shape((f, total), BF16),) * 3,
        us=7.6,
    )(cos, sin, pack, *parts)


def split(x, n):
    out = []
    for _ in range(n):
        h = x.astype(BF16)
        out.append(h)
        x = x - h.astype(F32)
    return out


def attend_kernel(q_ref, k_ref, v_ref, b_ref, o_ref, l_ref, ka, va, *, sub):
    S = k_ref.shape[1]
    bq = q_ref.shape[1]

    @pl.when(pl.program_id(1) == 0)
    def _():
        k = k_ref[...]
        ka[...] = jnp.concatenate([k, k, b_ref[...]], axis=0).T
        va[0:HEAD_DIM] = v_ref[...]
        va[HEAD_DIM:] = jnp.ones((16, S), BF16)

    high, low = split(q_ref[...].astype(F32) * (SCALE * LOG2E), 2)
    row = lax.broadcasted_iota(jnp.int32, (16, bq), 0)
    one = jnp.where(row == 0, 1.0, 0.0).astype(BF16)
    qa = jnp.concatenate([high, low, one], axis=0)
    steps = bq // sub

    def scores(i):
        return dot(ka[...], qa[:, i * sub : (i + 1) * sub], 1, 0)

    s = scores(0)
    for i in range(steps):
        later = scores(i + 1) if i + 1 < steps else None
        cols = slice(i * sub, (i + 1) * sub)
        top = jnp.max(s, axis=0, keepdims=True)
        p = jnp.exp2(s - top).astype(BF16)
        o = dot(va[...], p, 1, 0)
        total = o[HEAD_DIM : HEAD_DIM + 1]
        o_ref[:, cols] = (o[:HEAD_DIM] * (1.0 / total)).astype(BF16)
        l_ref[0, :, cols] = jnp.broadcast_to(top + jnp.log2(total), (8, sub))
        s = later


def attend_call(q, k, v, bias, first, count):
    S = q.shape[1]
    bq = S
    sub = min(256, S)
    whole = pl.BlockSpec((HEAD_DIM, S), lambda h, i: (h + first, 0))
    block = pl.BlockSpec((HEAD_DIM, bq), lambda h, i: (h + first, i))
    return call(
        functools.partial(attend_kernel, sub=sub),
        "attend",
        (shape((count * HEAD_DIM, S), BF16), shape((count, 8, S), F32)),
        grid=(count, S // bq),
        in_specs=[block, whole, whole, pl.BlockSpec((16, S), lambda h, i: (0, 0))],
        out_specs=(
            pl.BlockSpec((HEAD_DIM, bq), lambda h, i: (h, i)),
            pl.BlockSpec((1, 8, bq), lambda h, i: (h, 0, i)),
        ),
        scratch_shapes=[
            pltpu.VMEM((S, 2 * HEAD_DIM + 16), BF16),
            pltpu.VMEM((HEAD_DIM + 16, S), BF16),
        ],
        us=7.4 * count,
    )(q, k, v, bias)


def attend_back_kernel(
    q_ref, k_ref, v_ref, b_ref, o_ref, l_ref, g_ref, c_ref, s_ref, ck_ref, sk_ref,
    dq_ref, dk_ref, dv_ref, ka, va, dka, dva, *, sub
):
    S = k_ref.shape[1]
    bq = q_ref.shape[1]

    @pl.when(pl.program_id(1) == 0)
    def _():
        k = k_ref[...]
        one = jnp.ones((16, S), BF16)
        ka[...] = jnp.concatenate([k, k, b_ref[...], one], axis=0).T
        va[...] = jnp.concatenate([v_ref[...], one], axis=0).T
        dka[...] = jnp.zeros_like(dka)
        dva[...] = jnp.zeros_like(dva)

    q = q_ref[...].astype(F32) * SCALE
    qs = q.astype(BF16)
    high, low = split(q * LOG2E, 2)
    row = lax.broadcasted_iota(jnp.int32, (16, bq), 0)

    def spread(x):
        a, b, c = [y.astype(F32) for y in split(x, 3)]
        rest = jnp.where(row == 2, c, 0.0)
        return jnp.where(row == 0, a, jnp.where(row == 1, b, rest)).astype(BF16)

    one = jnp.where(row == 0, 1.0, 0.0).astype(BF16)
    g = g_ref[...]
    qa = jnp.concatenate([high, low, one, spread(-l_ref[0, 0:1])], axis=0)
    centre = jnp.sum(g.astype(F32) * o_ref[...].astype(F32), axis=0, keepdims=True)
    ga = jnp.concatenate([g, spread(-centre)], axis=0)
    for i in range(bq // sub):
        cols = slice(i * sub, (i + 1) * sub)
        p = jnp.exp2(dot(ka[...], qa[:, cols], 1, 0))
        p_low = p.astype(BF16)
        ds = (p * dot(va[...], ga[:, cols], 1, 0)).astype(BF16)
        dva[...] += dot(g[:, cols], p_low, 1, 1)
        dka[...] += dot(qs[:, cols], ds, 1, 1)
        dq = dot(k_ref[...], ds, 1, 0) * SCALE
        dq_ref[:, cols] = turn_back(dq, c_ref[:, cols], s_ref[:, cols]).astype(BF16)

    @pl.when(pl.program_id(1) == pl.num_programs(1) - 1)
    def _():
        dk_ref[...] = turn_back(dka[...], ck_ref[...], sk_ref[...]).astype(BF16)
        dv_ref[...] = dva[...].astype(BF16)


def attend_back_call(q, k, v, bias, o, lse, g, cos, sin, head, place):
    S = q.shape[1]
    bq = min(1024, S)
    half = HEAD_DIM // 2
    whole = pl.BlockSpec((HEAD_DIM, S), lambda h, i: (head, 0))
    block = pl.BlockSpec((HEAD_DIM, bq), lambda h, i: (head, i))
    table = pl.BlockSpec((half, S), lambda h, i: (0, 0))
    table_block = pl.BlockSpec((half, bq), lambda h, i: (0, i))
    return call(
        functools.partial(attend_back_kernel, sub=min(256, S)),
        "attend_back",
        (shape((HEAD_DIM, S), BF16),) * 3,
        us=12.3,
        grid=(1, S // bq),
        in_specs=[
            block, whole, whole,
            pl.BlockSpec((16, S), lambda h, i: (0, 0)),
            pl.BlockSpec((HEAD_DIM, bq), lambda h, i: (place, i)),
            pl.BlockSpec((1, 8, bq), lambda h, i: (place, 0, i)),
            block, table_block, table_block, table, table,
        ],
        out_specs=(
            pl.BlockSpec((HEAD_DIM, bq), lambda h, i: (0, i)),
            pl.BlockSpec((HEAD_DIM, S), lambda h, i: (0, 0)),
            pl.BlockSpec((HEAD_DIM, S), lambda h, i: (0, 0)),
        ),
        scratch_shapes=[
            pltpu.VMEM((S, 2 * HEAD_DIM + 32), BF16),
            pltpu.VMEM((S, HEAD_DIM + 16), BF16),
            pltpu.VMEM((HEAD_DIM, S), F32),
            pltpu.VMEM((HEAD_DIM, S), F32),
        ],
    )(q, k, v, bias, o, lse, g, cos, sin, cos, sin)


def stack_rows(refs, cols):
    return jnp.concatenate([r[:, cols] for r in refs], axis=0)


def out_kernel(n_heads, w_ref, *refs):
    heads, outs = refs[:n_heads], refs[n_heads:]
    n, d = outs[0].shape
    J, b = w_ref.shape[0], w_ref.shape[-1]
    for i, out in enumerate(outs):
        o = stack_rows(heads, slice(i * n, (i + 1) * n))
        for j in range(J):
            out[:, j * b : (j + 1) * b] = dot(o, w_ref[j], 0, 0).astype(BF16)


def pack_spec(pack, which):
    J, _, a, b = pack.shape
    return pl.BlockSpec((J, None, a, b), lambda i: (0, which, 0, 0))


def full(s):
    return pl.BlockSpec(s, lambda i: (0,) * len(s))


def out_call(heads, pack, n_parts, d):
    S = heads[0].shape[1]
    f = sum(o.shape[0] for o in heads)
    return call(
        functools.partial(out_kernel, len(heads)),
        "output_projection",
        (shape((S // n_parts, d), BF16),) * n_parts,
        grid=(1,),
        in_specs=[pack_spec(pack, 3)] + [full(o.shape) for o in heads],
        out_specs=(full((S // n_parts, d)),) * n_parts,
        us=4.2,
    )(pack, *heads)


def heads_grad_kernel(n_heads, n_parts, w_ref, *refs):
    heads, parts, (g_ref, dw_ref) = (
        refs[:n_heads], refs[n_heads : n_heads + n_parts], refs[n_heads + n_parts :]
    )
    n = parts[0].shape[0]
    J, b = w_ref.shape[0], w_ref.shape[-1]
    w = jnp.concatenate([w_ref[j] for j in range(J)], axis=1)
    total = None
    for i, p in enumerate(parts):
        cols = slice(i * n, (i + 1) * n)
        g_ref[:, cols] = dot(w, p[...], 1, 1).astype(BF16)
        term = dot(stack_rows(heads, cols), p[...], 1, 0)
        total = term if total is None else total + term
    for j in range(J):
        dw_ref[j] = total[:, j * b : (j + 1) * b].astype(BF16)


def heads_grad_call(heads, pack, parts):
    S = heads[0].shape[1]
    f = sum(o.shape[0] for o in heads)
    n, d = parts[0].shape
    J, _, a, b = pack.shape
    return call(
        functools.partial(heads_grad_kernel, len(heads), len(parts)),
        "heads_grad",
        (shape((f, S), BF16), shape((J, a, b), BF16)),
        grid=(1,),
        in_specs=[pack_spec(pack, 3)] + [full(o.shape) for o in heads] + [full((n, d))] * len(parts),
        out_specs=(full((f, S)), full((J, a, b))),
        us=6,
    )(pack, *heads, *parts)


def qkv_back_kernel(n_parts, n_groups, w_ref, *refs):
    grads, outs = refs[: 3 * n_groups], refs[3 * n_groups :]
    n, d = outs[0].shape
    f = w_ref.shape[-1]
    for i, out in enumerate(outs):
        cols = slice(i * n, (i + 1) * n)
        total = None
        for j in range(3):
            g = stack_rows(grads[j::3], cols)
            term = dot(g, w_ref[:, j].reshape(d, f), 0, 1)
            total = term if total is None else total + term
        out[...] = total.astype(BF16)


def qkv_back_call(pack, grads, n_parts, d):
    f = pack.shape[-1]
    S = grads[0][0].shape[1]
    flat = [g for group in grads for g in group]
    return call(
        functools.partial(qkv_back_kernel, n_parts, len(grads)),
        "qkv_back",
        (shape((S // n_parts, d), BF16),) * n_parts,
        us=7,
    )(pack, *flat)


def qkv_weight_kernel(n_parts, n_groups, J, index_ref, wo_ref, *refs):
    grads, parts = refs[: 3 * n_groups], refs[3 * n_groups : 3 * n_groups + n_parts]
    outs, held = refs[3 * n_groups + n_parts : -1], refs[-1]
    n = parts[0].shape[0]
    a = outs[0].shape[1]
    for j in range(3):
        total = None
        for i, p in enumerate(parts):
            g = stack_rows(grads[j::3], part_cols(i, n_parts, n))
            term = dot(p[...], g, 0, 1)
            total = term if total is None else total + term
        held[...] = total.astype(BF16).reshape(held.shape)
        for k in range(J):
            outs[k][j] = held[index_ref[k]]
    for k in range(J):
        outs[k][3] = wo_ref[index_ref[k]]


def qkv_weight_call(index, wo_grad, grads, parts, pack_shape):
    J, four, a, b = pack_shape
    flat = [g for group in grads for g in group]
    vmem = pl.BlockSpec(memory_space=pltpu.VMEM)
    return call(
        functools.partial(qkv_weight_kernel, len(parts), len(grads), J),
        "qkv_weights",
        (shape((four, a, b), BF16),) * J,
        us=8,
        in_specs=[pl.BlockSpec(memory_space=pltpu.SMEM)] + [vmem] * (1 + len(flat) + len(parts)),
        out_specs=(vmem,) * J,
        scratch_shapes=[pltpu.VMEM((J, a, b), BF16)],
    )(index, wo_grad, *flat, *parts)


def pack_kernel(n_parts, index_ref, q_ref, o_ref, *refs):
    parts, out = refs[:-1], refs[-1]
    J, _, a, b = out.shape

    @pl.when(index_ref[n_parts] == 0)
    def _():
        for j in range(J):
            for which in range(3):
                out[j, which] = q_ref[which, j * a : (j + 1) * a]
            out[j, 3] = o_ref[:, j * b : (j + 1) * b]

    @pl.when(index_ref[n_parts] == 1)
    def _():
        for i, p in enumerate(parts):
            out[index_ref[i]] = p[...]


def pack_call(index, wq, wo, parts):
    _, a, b = parts[0].shape
    J = len(parts)
    vmem = pl.BlockSpec(memory_space=pltpu.VMEM)
    return call(
        functools.partial(pack_kernel, J),
        "pack_heads",
        shape((J, 4, a, b), BF16),
        in_specs=[pl.BlockSpec(memory_space=pltpu.SMEM)] + [vmem] * (J + 2),
        out_specs=vmem,
        us=3.7,
    )(index, wq, wo, *parts)


def column_sums(x):
    return jnp.sum(x.T, axis=0, keepdims=True)


def unpack_kernel(n_parts, index_ref, w_ref, *refs):
    parts, (q_ref, o_ref, gain_ref) = refs[:n_parts], refs[n_parts:]
    a, b = parts[0].shape[1:]
    for i, p in enumerate(parts):
        j = index_ref[i]
        rows = pl.ds(pl.multiple_of(j * a, a), a)
        gain = None
        for which in range(3):
            g = p[which].astype(F32)
            q_ref[which, rows, :] = g
            term = g * w_ref[which, rows, :].astype(F32)
            gain = term if gain is None else gain + term
        o_ref[:, pl.ds(pl.multiple_of(j * b, b), b)] = p[3].astype(F32)
        gain_ref[:, rows] = column_sums(gain)


def unpack_call(index, wq, parts):
    _, a, b = parts[0].shape
    J = len(parts)
    vmem = pl.BlockSpec(memory_space=pltpu.VMEM)
    return call(
        functools.partial(unpack_kernel, J),
        "unpack_heads",
        (shape((3, J * a, b), F32), shape((a, J * b), F32), shape((1, J * a), F32)),
        in_specs=[pl.BlockSpec(memory_space=pltpu.SMEM)] + [vmem] * (J + 1),
        out_specs=(vmem, vmem, vmem),
        us=3.8,
    )(index, wq, *parts)


def ffn_kernel(groups, steps, *refs):
    x0, x1, c0, c1 = refs[:4]
    weights = refs[4 : 4 + 3 * groups]
    h_ref, gl_ref, ul_ref, out0, out1, dx0, dx1 = refs[4 + 3 * groups :]
    early = pl.program_id(0) < steps
    x = jnp.where(early, x0[...], x1[...])
    c = jnp.where(early, c0[...], c1[...])
    out = dx = None
    for m in range(groups):
        wg, wu, wd = [r[...].reshape(-1, r.shape[-1]) for r in weights[3 * m : 3 * m + 3]]
        gate = dot(x, wg, 1, 1)
        up = dot(x, wu, 1, 1)
        hg = dot(c, wd, 1, 1)
        sig = jax.nn.sigmoid(gate)
        act = gate * sig
        hidden = (act * up).astype(BF16)
        gl = (hg * up * (sig * (1.0 + gate * (1.0 - sig)))).astype(BF16)
        ul = (hg * act).astype(BF16)
        cols = slice(m * wg.shape[0], (m + 1) * wg.shape[0])
        h_ref[:, cols] = hidden
        gl_ref[:, cols] = gl
        ul_ref[:, cols] = ul
        o = dot(hidden, wd, 1, 0)
        e = dot(gl, wg, 1, 0) + dot(ul, wu, 1, 0)
        out = o if out is None else out + o
        dx = e if dx is None else dx + e

    @pl.when(early)
    def _():
        out0[...] = out.astype(BF16)
        dx0[...] = dx.astype(BF16)

    @pl.when(jnp.logical_not(early))
    def _():
        out1[...] = out.astype(BF16)
        dx1[...] = dx.astype(BF16)


def ffn_call(xs, cs, weights):
    n, d = xs[0].shape
    groups = len(weights)
    T, us, _ = weights[0][0].shape
    units = groups * T * us
    b = min(256, n)
    steps = n // b
    first = pl.BlockSpec((b, d), lambda i: (jnp.minimum(i, steps - 1), 0))
    second = pl.BlockSpec((b, d), lambda i: (jnp.maximum(i - steps, 0), 0))
    urow = pl.BlockSpec((b, units), lambda i: (i, 0))
    specs, args = [], []
    for group in weights:
        specs += [pl.BlockSpec((T, us, d), lambda i: (0, 0, 0))] * 3
        args += group
    return call(
        functools.partial(ffn_kernel, groups, steps),
        "feed_forward",
        (shape((2 * n, units), BF16),) * 3 + (shape((n, d), BF16),) * 4,
        grid=(2 * steps,),
        in_specs=[first, second, first, second] + specs,
        out_specs=(urow,) * 3 + (first, second, first, second),
        us=21,
    )(*xs, *cs, *args)


def ffn_weight_kernel(T, us, *refs):
    x, c = refs[:4], refs[4:8]
    h, gl, ul = refs[8:10], refs[10:12], refs[12:14]
    outs = refs[14:]
    n = x[0].shape[0]

    def product(a, b):
        total = None
        for i in range(4):
            rows = slice((i % 2) * n, (i % 2 + 1) * n)
            term = dot(a[i][...], b(i, rows), 0, 0)
            total = term if total is None else total + term
        return total.astype(BF16)

    dw = product(c, lambda i, rows: h[i // 2][rows])
    for t in range(T):
        outs[0][t, 2] = dw[:, t * us : (t + 1) * us]
    dw = product(x, lambda i, rows: jnp.concatenate([gl[i // 2][rows], ul[i // 2][rows]], axis=1))
    for j in range(2):
        for t in range(T):
            at = (j * T + t) * us
            outs[0][t, j] = dw[:, at : at + us]


def ffn_weight_call(x, c, h, gl, ul, m, T, us):
    n, d = x[0].shape
    db = min(256, d)
    spec = [pl.BlockSpec((n, db), lambda i: (0, i))] * 8
    spec += [pl.BlockSpec((2 * n, T * us), lambda i: (0, m))] * 6
    return call(
        functools.partial(ffn_weight_kernel, T, us),
        "feed_forward_weights",
        shape((T, 3, d, us), BF16),
        grid=(d // db,),
        in_specs=spec,
        out_specs=pl.BlockSpec((T, 3, db, us), lambda i: (0, 0, i, 0)),
        us=12.4,
    )(*x, *c, *h, *gl, *ul)


def assemble_kernel(w_ref, old_ref, gu_ref, dn_ref, gain_ref):
    DP, _, _, us = w_ref.shape
    gain = None
    for j in range(2):
        rows = jnp.concatenate([w_ref[p, j] for p in range(DP)], axis=1).astype(F32)
        gu_ref[:, j, :] = rows
        term = rows * old_ref[:, j, :].astype(F32)
        gain = term if gain is None else gain + term
    gain_ref[...] = column_sums(gain)
    rows = jnp.concatenate([w_ref[p, 2] for p in range(DP)], axis=1)
    dn_ref[...] = rows.T.astype(F32)


def assemble_call(w, old):
    DP, _, d, us = w.shape
    b = min(256, d)
    return call(
        assemble_kernel,
        "feed_forward_gradients",
        (shape((d, 2, DP * us), F32), shape((DP * us, d), F32), shape((1, d), F32)),
        us=9,
        grid=(d // b,),
        in_specs=[
            pl.BlockSpec((DP, 3, b, us), lambda i: (0, 0, i, 0)),
            pl.BlockSpec((b, 2, DP * us), lambda i: (i, 0, 0)),
        ],
        out_specs=(
            pl.BlockSpec((b, 2, DP * us), lambda i: (i, 0, 0)),
            pl.BlockSpec((DP * us, b), lambda i: (0, i)),
            pl.BlockSpec((1, b), lambda i: (0, i)),
        ),
    )(w, old)


def after(x, *deps):
    return lax.optimization_barrier((x, *deps))[0]


def tie(*xs):
    return lax.optimization_barrier(xs)


def build(DP, T):
    M = DP // 4
    R = T // 2
    J = DP // 2

    def over_dp(x, f):
        return lax.ppermute(x, "dp", [(i, f(i)) for i in range(DP)])

    def core_flip(x):
        return over_dp(x, lambda i: i ^ 1)

    def top_flip(x):
        return over_dp(x, lambda i: (i + DP // 2) % DP)

    def mid_from(x, k):
        def dest(i):
            a, m, c = i // (DP // 2), (i // 2) % M, i % 2
            return a * (DP // 2) + ((m - k) % M) * 2 + c

        return over_dp(x, dest)

    def pair_from(x, k):
        return over_dp(x, lambda i: ((i // 2) ^ k) * 2 + i % 2)

    def row_from(x, k):
        return lax.ppermute(
            x, "tensor", [((t // R) * R + (t % R + k) % R, t) for t in range(T)]
        )

    def reshard(x):
        pairs = []
        for d in range(DP):
            for t in range(T):
                j, c, h, r = d // 2, d % 2, t // R, t % R
                pairs.append((d * T + t, (2 * j + h) * T + c * R + r))
        return lax.ppermute(x, ("dp", "tensor"), pairs)

    def send_rows(x):
        return [row_from(x, k) for k in range(1, R)]

    def gather_heads(x, flipped, rows, hold):
        out = [x, flipped]
        for y in rows:
            y = after(y, hold)
            out += [y, core_flip(y)]
        return out

    def sum_heads(pieces):
        flips = [core_flip(z) for z in pieces[1::2]]
        sums = [
            (pieces[2 * k].astype(F32) + flips[k].astype(F32)).astype(BF16) for k in range(1, R)
        ]
        return sums, [pieces[0], flips[0]]

    def scatter_heads(pieces):
        out = []
        for k in range(R):
            mine, theirs = pieces[2 * k], core_flip(pieces[2 * k + 1])
            if k == 0:
                out += [mine, theirs]
            else:
                both = (mine.astype(F32) + theirs.astype(F32)).astype(BF16)
                out.append(row_from(both, R - k))
        return out

    def gather_units(y):
        z = top_flip(y)
        return [y, core_flip(y), z, core_flip(z)]

    def sum_rows(x):
        for bit in range(T.bit_length() - 1):
            x = x + lax.ppermute(x, "tensor", [(t, t ^ (1 << bit)) for t in range(T)])
        return x

    def on_device(
        tokens, qkv_weight, output_projection_weight, gate_up_weight, down_projection_weight,
        attention_gain, feedforward_gain, window_lengths, key_mask, cotangent,
    ):
        n, _, d = tokens.shape
        length = key_mask.shape[0]
        me_d, me_t = lax.axis_index("dp"), lax.axis_index("tensor")
        core, h, r, pair = me_d % 2, me_t // R, me_t % R, me_d // 2
        us = down_projection_weight.shape[0] // DP
        gain_one, gain_two = attention_gain[None], feedforward_gain[None]
        a = d // J

        xs = [reshard(tokens[i * n // 2 : (i + 1) * n // 2, 0]) for i in (0, 1)]

        wq_own = qkv_weight.transpose(1, 0, 2)
        f = wq_own.shape[2]
        share = jnp.concatenate(
            [
                lax.dynamic_slice_in_dim(wq_own, pair * a, a, 1),
                lax.dynamic_slice_in_dim(output_projection_weight, pair * a, a, 1)[None],
            ],
            axis=0,
        )
        far_pairs = [
            ((2 * j + 1) * T + t, (2 * j + 1) * T + (t + R) % T)
            for j in range(J)
            for t in range(T)
        ]
        share = lax.ppermute(after(share, xs[0]), ("dp", "tensor"), far_pairs)
        shares = [share] + [
            lax.ppermute(
                share, "dp", [(2 * j + 1, 2 * (j ^ k) + 1) for j in range(J)]
            )
            for k in range(1, J)
        ]
        index = jnp.stack([pair ^ k for k in range(J)] + [core]).astype(jnp.int32)
        pack = pack_call(index, wq_own, output_projection_weight, shares)

        positions = jnp.arange(length, dtype=jnp.int32)
        valid = (positions < window_lengths[0]) & (key_mask[:, 0] == 1)
        bias_own = jnp.where(valid, 0.0, MASKED).astype(F32)
        bias = jnp.where(core == h, bias_own, core_flip(bias_own))
        order = jnp.stack(
            [((core + dc) % 2) * R + (r + dr) % R for dr in range(R) for dc in (0, 1)]
        )
        bias = jnp.take(bias.reshape(T, n), order, axis=0).reshape(length)
        bias = jnp.concatenate(
            [bias[None].astype(BF16), jnp.zeros((15, length), BF16)], axis=0
        )
        places = (order[:, None] * n + jnp.arange(n, dtype=jnp.int32)[None]).reshape(length)
        half = HEAD_DIM // 2
        frequencies = ROPE_BASE ** (-(jnp.arange(half, dtype=F32) * 2.0 / HEAD_DIM))
        angles = frequencies[:, None] * places.astype(F32)[None]
        cos, sin = jnp.cos(angles), jnp.sin(angles)

        gate, up = lax.dynamic_slice_in_dim(gate_up_weight, me_d * us, us, 2).transpose(1, 2, 0)
        dn = lax.dynamic_slice_in_dim(down_projection_weight, me_d * us, us, 0)

        xs[0], _ = lax.optimization_barrier((xs[0], (bias, cos, sin, gate, up, index)))
        first = norm_call(xs[0], gain_one)
        rows_one = send_rows(first)
        second = norm_call(after(xs[1], first), gain_one)
        rows_two = send_rows(second)
        flips = [core_flip(first), core_flip(second)]
        normed_one = gather_heads(first, flips[0], rows_one, second)
        normed_one += gather_heads(second, flips[1], rows_two, pack)
        x = jnp.concatenate(xs)
        cot = reshard(after(cotangent[:, 0], xs[1]))

        gate, up, dn = [
            lax.all_gather(z, "tensor", axis=0) for z in tie(gate, up, dn, second)[:3]
        ]
        own_units = (gate, up, dn)
        weights = [own_units] + [[mid_from(z, k) for z in own_units] for k in range(1, M)]
        q, k, v = qkv_call(normed_one, pack, cos, sin)
        heads = f // HEAD_DIM
        count = heads
        o, lse = [], []
        for first in range(0, heads, count):
            if first:
                q, o[0] = tie(q, o[0])
            got = attend_call(q, k, v, bias, first, count)
            o.append(got[0])
            lse.append(got[1])
        o[-1], cot = tie(o[-1], cot)
        pieces = out_call(o, pack, T, d)
        cots = gather_units(after(cot, pieces[0]))
        arrived = scatter_heads(pieces)
        middle, normed = middle_call(x, gain_two, arrived)

        xs = gather_units(normed)
        near = ffn_call(xs[:2], cots[:2], weights)
        near_dx = core_flip(near[6])
        far = ffn_call([after(xs[2], near[0]), xs[3]], cots[2:], weights)

        def core_sum(mine, theirs):
            return (mine.astype(F32) + core_flip(theirs).astype(F32)).astype(BF16)

        dx_both = core_sum(far[5], far[6])
        crossed = top_flip(dx_both)

        def weight_grads(m, hold):
            return ffn_weight_call(
                [after(xs[0], hold), *xs[1:]], cots, *[[near[i], far[i]] for i in range(3)], m, T, us
            )

        sent, hold = [], dx_both
        for m in range(M - 1, 0, -1):
            hold = weight_grads(m, hold)
            sent.append(mid_from(hold, M - m))
        out_both = core_sum(after(far[3], hold), far[4])
        near_out = core_flip(after(near[4], hold))
        crossed, out_both, near_out = tie(crossed, out_both, near_out)
        middle_grad, middle_low = back_call(
            "middle_grad", cot, middle, gain_two, [near[5], near_dx, crossed], 1
        )
        low_rows = send_rows(middle_low)
        out_crossed = top_flip(out_both)
        flipped = core_flip(middle_low)
        own_grads = weight_grads(0, flipped)
        output = output_call(after(middle, own_grads), [near[3], near_out, out_crossed])
        lows = gather_heads(middle_low, flipped, low_rows, output)
        moved_output = reshard(output)
        g, wo_grad = heads_grad_call(o, pack, lows)

        back = []
        for i in range(heads):
            if i == 1:
                total = after(own_grads, back[0][0]).astype(F32)
                for z in sent:
                    total = total + z.astype(F32)
                total = total.astype(BF16)
                g, total, moved_output = tie(g, total, moved_output)
                slices = lax.psum_scatter(total, "tensor", scatter_dimension=0)
            elif i:
                g = after(g, back[-1][0])
            j = i // count
            back.append(
                attend_back_call(q, k, v, bias, o[j], lse[j], g, cos, sin, i, i - j * count)
            )
        pieces = qkv_back_call(after(pack, back[-1][0]), back, T, d)
        sums, mine = sum_heads(pieces)
        rows = [row_from(z, R - k) for k, z in enumerate(sums, 1)]
        wo_grad, *sums = tie(wo_grad, *sums)
        dw = qkv_weight_call(index, wo_grad, back, normed_one, pack.shape)

        travelled = [pair_from(dw[k], k) for k in range(1, J)]
        slices, share = tie(slices, dw[0])
        slices = lax.all_gather(slices, "dp", axis=0)
        tokens_low = back_call(
            "tokens_grad", middle_grad, after(x, share), gain_one, mine + rows, 0
        )[0]
        tokens_grad = reshard(tokens_low)[:, None]
        tokens_low, *travelled = tie(tokens_low, *travelled)
        part = share.astype(F32)
        for p in travelled:
            part = part + p.astype(F32)
        part = part.astype(BF16)
        home_pairs = [
            ((2 * j + 1) * T + t, 2 * j * T + (t + R) % T) for j in range(J) for t in range(T)
        ]
        moved = lax.ppermute(part, ("dp", "tensor"), home_pairs)
        part = (part.astype(F32) + moved.astype(F32)).astype(BF16)
        part = jnp.where(core == 0, part, core_flip(part))
        shares = [part] + [pair_from(part, k) for k in range(1, J)]

        gate_up_grad, down_grad, gain_two_part = assemble_call(
            after(slices, part), gate_up_weight
        )
        qkv_grad, out_grad, gain_one_part = unpack_call(after(index, down_grad), wq_own, shares)
        qkv_grad = qkv_grad.transpose(1, 0, 2)
        gains = sum_rows(jnp.concatenate([gain_one_part, gain_two_part], axis=0))
        gains = gains / jnp.concatenate([gain_one, gain_two], axis=0)
        return (
            moved_output[:, None], tokens_grad, qkv_grad, out_grad, gate_up_grad, down_grad, gains[0], gains[1]
        )

    return on_device


def solution(mesh):
    return jax.shard_map(
        build(mesh.shape["dp"], mesh.shape["tensor"]),
        mesh=mesh,
        in_specs=(
            P("tensor", "dp", None),
            P(None, None, "tensor"),
            P("tensor", None),
            P(None, None, "tensor"),
            P("tensor", None),
            P(),
            P(),
            P("dp"),
            P(None, "dp"),
            P("tensor", "dp", None),
        ),
        out_specs=(
            P("tensor", "dp", None),
            P("tensor", "dp", None),
            P(None, None, "tensor"),
            P("tensor", None),
            P(None, None, "tensor"),
            P("tensor", None),
            P(),
            P(),
        ),
        check_vma=False,
    )
```
